256 devices in a mesh: query: 8 (over y, core), passage: 32 (over x, z).
Axes of the slice: x: 4, y: 4, z: 8, core: 2. Of those that a mesh axis runs over, the one named last changes fastest.
Arguments:
- tokens: bfloat16 [4096, 32, 768], P(('query', 'passage')), may hold values from -6 to 6
- weight_in: bfloat16 [768, 3072], replicated, may hold values from -0.21875 to 0.21875
- bias_in: float32 [3072], replicated, may hold values from -3 to 3
- weight_out: bfloat16 [3072, 768], replicated, may hold values from -0.109375 to 0.109375
- bias_out: float32 [768], replicated, may hold values from -3 to 3
- norm_gain: float32 [768], replicated, may hold values from 0.5 to 1.5
- norm_shift: float32 [768], replicated, may hold values from -2 to 2
- projection: bfloat16 [768, 128], replicated, may hold values from -0.21875 to 0.21875
- tiles: bfloat16 [384, 128, 128], P('passage'), may hold values from -0.5 to 0.5
- lengths: int32 [384], P('passage'), may hold values from 16 to 128
- slots: int32 [4096, 32, 4], P('query', 'passage'), may hold values from 0 to 11
- counts: int32 [4096, 32], P('query', 'passage'), may hold values from 0 to 4
Outputs:
- scores: float32 [4096, 32, 4], P(('query', 'passage'))
The draws below stay inside these ranges and needn't reach their ends.
Inputs may be any that keep to these rules, and one draw needn't show every extreme that they name: `slots`: slot of a candidate tile among the 12 tiles of its shard. slots c with c >= counts[q, s] are unused. Positions j >= lengths[t] of a tile are padding.
All inputs are finite; a program needn't handle non-finite values.
Results may differ from the reference program's by a relative error of at most 0.0004.
Values may be sent and summed in bfloat16 or wider, within the bound.
No kernel may reach another device: no remote copies, remote signals or barrier semaphores. Data moves between devices by JAX's collectives and lax.ppermute only.
A program may use at most 64 MiB of HBM per device.

```python
import jax
import jax.numpy as jnp
from jax import lax

D = 768
FF = 3072
EMB = 128
QLEN = 32
TILE = 128
CAP = 4
Q_DEV = 16
TILES_DEV = 12
SHARDS = 32
QUERIES = 4096
NTILES = 384


def touch_ends(array, key, smallest, high):
    index_at = [jax.random.randint(jax.random.fold_in(key, axis), (), 0, length) for axis, length in enumerate(array.shape)]
    longest = array.shape.index(max(array.shape))
    next_to = index_at[:longest] + [(index_at[longest] + 1) % array.shape[longest]] + index_at[longest + 1:]
    return array.at[tuple(index_at)].set(smallest).at[tuple(next_to)].set(high)


def steps_of(key, shape, cuts, least, top_value):
    def one(dim, parts):
        steps = jax.random.uniform(jax.random.fold_in(jax.random.fold_in(key, 6), dim), (parts,), jnp.float32, least / len(cuts), top_value / len(cuts))
        return jnp.repeat(jnp.exp(steps), shape[dim] // parts).reshape((-1,) + (1,) * (len(shape) - dim - 1))

    loudness = one(*cuts[0])
    for cut in cuts[1:]:
        loudness = loudness * one(*cut)
    return loudness


def scatter_about(own_key, dims, deviation, reach, cuts=(), held_as=jnp.bfloat16):
    loudness = steps_of(own_key, dims, cuts, -0.22, 0.18) if cuts else 1.0
    drawn = jax.random.normal(own_key, dims, jnp.float32) * deviation * loudness
    return jnp.minimum(jnp.maximum(drawn, -reach), reach).astype(held_as)


def setup_inputs(seed: int = 0) -> dict:
    streams_of = jax.random.split(jax.random.key(seed), 13)
    tokens = scatter_about(streams_of[0], (QUERIES, QLEN, D), 1.0, 6.0, ((0, 256),))
    weight_in = scatter_about(streams_of[1], (D, FF), D ** -0.5, 0.21875)
    bias_in = scatter_about(streams_of[2], (FF,), 0.5, 3.0, (), jnp.float32)
    weight_out = scatter_about(streams_of[3], (FF, D), FF ** -0.5, 0.109375)
    bias_out = scatter_about(streams_of[4], (D,), 0.5, 3.0, (), jnp.float32)
    norm_gain = jnp.clip(1.0 + 0.1 * jax.random.normal(streams_of[5], (D,), jnp.float32), 0.5, 1.5)
    norm_shift = scatter_about(streams_of[6], (D,), 0.3, 2.0, (), jnp.float32)
    projection = scatter_about(streams_of[7], (D, EMB), D ** -0.5, 0.21875)
    tiles = scatter_about(streams_of[8], (NTILES, TILE, EMB), 0.0884, 0.5, ((0, 32),))
    lengths = touch_ends(jax.random.randint(streams_of[9], (NTILES,), TILE // 8, TILE + 1), jax.random.fold_in(streams_of[9], 1), TILE // 8, TILE).astype(jnp.int32)
    slots = touch_ends(jax.random.randint(streams_of[10], (QUERIES, SHARDS, CAP), 0, TILES_DEV), jax.random.fold_in(streams_of[10], 1), 0, TILES_DEV - 1).astype(jnp.int32)
    counts = touch_ends(jax.random.randint(streams_of[11], (QUERIES, SHARDS), 0, CAP + 1), jax.random.fold_in(streams_of[11], 1), 0, CAP).astype(jnp.int32)
    return {"tokens": tokens, "weight_in": weight_in, "bias_in": bias_in, "weight_out": weight_out, "bias_out": bias_out, "norm_gain": norm_gain, "norm_shift": norm_shift, "projection": projection, "tiles": tiles, "lengths": lengths, "slots": slots, "counts": counts}


def encode(block, weight_in, bias_in, weight_out, bias_out, norm_gain, norm_shift, projection):
    pre = jnp.dot(block, weight_in, preferred_element_type=jnp.float32) + bias_in
    hidden = jax.nn.gelu(pre, approximate=False).astype(jnp.bfloat16)
    total = jnp.dot(hidden, weight_out, preferred_element_type=jnp.float32) + bias_out + block.astype(jnp.float32)
    center = lax.optimization_barrier(jnp.mean(total, axis=-1, keepdims=True))
    spread = lax.optimization_barrier(jnp.mean((total - center) ** 2, axis=-1, keepdims=True))
    normed = ((total - center) / jnp.sqrt(spread + 1e-05) * norm_gain + norm_shift).astype(jnp.bfloat16)
    projected = jnp.dot(normed, projection, preferred_element_type=jnp.float32)
    scale = 1.0 / jnp.sqrt(lax.optimization_barrier(jnp.sum(projected * projected, axis=-1, keepdims=True)) + 1e-06)
    return (projected * scale).astype(jnp.bfloat16)

def reference(tokens, weight_in, bias_in, weight_out, bias_out, norm_gain, norm_shift, projection, tiles, lengths, slots, counts):
    blocks = QUERIES // Q_DEV
    flat = tokens.reshape(blocks, Q_DEV * QLEN, D)

    def encode_block(block):
        return encode(block, weight_in, bias_in, weight_out, bias_out, norm_gain, norm_shift, projection)
    embeds = lax.map(encode_block, flat).reshape(blocks, Q_DEV, QLEN, EMB)
    offsets = (jnp.arange(SHARDS, dtype=jnp.int32) * TILES_DEV)[None, :, None]

    def score_block(inputs):
        query_emb, slot_block, count_block = inputs
        chosen = (slot_block + offsets).astype(jnp.int32)
        picked = tiles[chosen].astype(jnp.float32)
        picked_len = lengths[chosen]
        similar = jnp.einsum('qid,qsctd->qscit', query_emb.astype(jnp.float32), picked)
        position = jnp.arange(TILE, dtype=jnp.int32)
        mask = position[None, None, None, None, :] < picked_len[:, :, :, None, None]
        best = lax.optimization_barrier(jnp.max(jnp.where(mask, similar, jnp.float32(-1e+30)), axis=-1))
        summed = lax.optimization_barrier(jnp.sum(best, axis=-1))
        valid = jnp.arange(CAP, dtype=jnp.int32)[None, None, :] < count_block[:, :, None]
        return jnp.where(valid, summed, jnp.float32(0.0))
    slot_blocks = slots.reshape(blocks, Q_DEV, SHARDS, CAP)
    count_blocks = counts.reshape(blocks, Q_DEV, SHARDS)
    result = lax.map(score_block, (embeds, slot_blocks, count_blocks))
    return result.reshape(QUERIES, SHARDS, CAP)
```

```python
import functools

import jax
import jax.numpy as jnp
from jax import lax
from jax.experimental import pallas as pl
from jax.experimental.pallas import tpu as pltpu
from jax.sharding import Mesh
from jax.sharding import PartitionSpec as P

Y, CORES, X, Z = 4, 2, 4, 8
HALF_ROOT = 0.7071067811865476


def turn(size, step):
    return [(i, (i + step) % size) for i in range(size)]


def gelu(pre):
    return 0.5 * pre * (1.0 + lax.erf(pre * jnp.float32(HALF_ROOT)))


def ffn_part(tok, w_in, b_in, w_out):
    pre = jnp.dot(tok[...], w_in[...], preferred_element_type=jnp.float32) + b_in[...]
    hidden = gelu(pre).astype(jnp.bfloat16)
    return jnp.dot(hidden, w_out[...], preferred_element_type=jnp.float32)


def ffn_first(tok, w_in, b_in, w_out, acc):
    part = ffn_part(tok, w_in, b_in, w_out)

    @pl.when(pl.program_id(0) == 0)
    def _():
        acc[...] = part

    @pl.when(pl.program_id(0) > 0)
    def _():
        acc[...] += part


def ffn_second(tok, w_in, b_in, w_out, begun, b_out, gain, shift, proj, out, acc, turned, *, queries, tokens):
    part = ffn_part(tok, w_in, b_in, w_out)

    @pl.when(pl.program_id(0) == 0)
    def _():
        acc[...] = begun[...] + part

    @pl.when(pl.program_id(0) > 0)
    def _():
        acc[...] += part

    @pl.when(pl.program_id(0) == pl.num_programs(0) - 1)
    def _():
        total = acc[...] + b_out[...] + tok[...].astype(jnp.float32)
        diff = total - jnp.mean(total, axis=-1, keepdims=True)
        spread = jnp.mean(diff * diff, axis=-1, keepdims=True)
        normed = (diff * lax.rsqrt(spread + 1e-5) * gain[...] + shift[...]).astype(jnp.bfloat16)
        projected = jnp.dot(normed, proj[...], preferred_element_type=jnp.float32)
        scale = lax.rsqrt(jnp.sum(projected * projected, axis=-1, keepdims=True) + 1e-6)
        embeds = projected * scale
        for q in range(queries):
            turned[pl.ds(q, tokens, stride=queries), :] = embeds[q * tokens : (q + 1) * tokens, :]
        out[...] = turned[...].astype(jnp.bfloat16)


def encode(tok, w_in, b_in, w_out, b_out, gain, shift, proj, queries, tokens, chunk=768):
    rows, width = tok.shape
    steps = w_in.shape[1] // chunk
    first = steps // 2
    params = pltpu.CompilerParams(vmem_limit_bytes=40 << 20)

    def whole(a):
        return pl.BlockSpec(a.shape, lambda j: (0,) * a.ndim)

    def pieces(skip):
        return [
            whole(tok),
            pl.BlockSpec((width, chunk), lambda j: (0, j + skip)),
            pl.BlockSpec((1, chunk), lambda j: (0, j + skip)),
            pl.BlockSpec((chunk, width), lambda j: (j + skip, 0)),
        ]

    def cost(n):
        return pl.CostEstimate(flops=4 * rows * width * chunk * n, bytes_accessed=4 * width * chunk * n, transcendentals=0)

    begun = pl.pallas_call(
        ffn_first,
        grid=(first,),
        in_specs=pieces(0),
        out_specs=pl.BlockSpec((rows, width), lambda j: (0, 0)),
        out_shape=jax.ShapeDtypeStruct((rows, width), jnp.float32),
        compiler_params=params,
        cost_estimate=cost(first),
        name="ffn_first",
    )(tok, w_in, b_in, w_out)
    return begun, lambda begun: pl.pallas_call(
        functools.partial(ffn_second, queries=queries, tokens=tokens),
        grid=(steps - first,),
        in_specs=pieces(first) + [whole(begun), whole(b_out), whole(gain), whole(shift), whole(proj)],
        out_specs=pl.BlockSpec((rows, proj.shape[1]), lambda j: (0, 0)),
        out_shape=jax.ShapeDtypeStruct((rows, proj.shape[1]), jnp.bfloat16),
        scratch_shapes=[pltpu.VMEM((rows, width), jnp.float32), pltpu.VMEM((rows, proj.shape[1]), jnp.float32)],
        compiler_params=params,
        cost_estimate=cost(steps - first),
        name="ffn_second",
    )(tok, w_in, b_in, w_out, begun, b_out, gain, shift, proj)


def score_kernel(place, mine, other, *refs, tiles, length, group):
    parcels, out, acc = refs[:-2], refs[-2], refs[-1]
    rows = tiles * length
    lane_group = lax.broadcasted_iota(jnp.int32, (8, 128), 1) // group
    for side, queries in enumerate((mine, other)):

        def one(step, _, queries=queries, side=side):
            start = pl.multiple_of(step * 512, 512)
            block = queries[pl.ds(start, 512), :]
            here = lane_group == place[side * 4 + step]
            for n, parcel in enumerate(parcels):
                similar = lax.dot_general(
                    parcel[0:rows, :], block, (((1,), (1,)), ((), ())), preferred_element_type=jnp.float32
                )
                sums = []
                for t in range(tiles):
                    best = jnp.max(similar[t * length : (t + 1) * length], axis=0, keepdims=True)
                    sums.append(best[:, 0:128] + best[:, 128:256] + best[:, 256:384] + best[:, 384:512])
                sums = jnp.concatenate(sums + [jnp.zeros((8 - tiles, 128), jnp.float32)], axis=0)
                sums = sums + pltpu.roll(sums, 64, 1)
                sums = sums + pltpu.roll(sums, 32, 1)
                sums = sums + pltpu.roll(sums, 16, 1)
                acc[n] = jnp.where(here, sums, acc[n])
            return 0

        lax.fori_loop(0, 4, one, 0)
    own_z, first_tile = place[8], place[9]
    row = lax.broadcasted_iota(jnp.int32, (8, 128), 0)
    for n, parcel in enumerate(parcels):
        codes = parcel[rows : rows + 32, :].astype(jnp.float32)
        lines = []
        for c in range(4):
            code = jnp.sum(jnp.where(row == own_z, codes[c * 8 : c * 8 + 8], 0.0), axis=0, keepdims=True)
            picked = code.astype(jnp.int32) - first_tile == row
            lines.append(jnp.sum(jnp.where(picked & (row < tiles), acc[n], 0.0), axis=0, keepdims=True))
        out[n] = jnp.concatenate(lines, axis=0)


def score(place, mine, other, parcels, tiles, length, group):
    n = len(parcels)
    vm = pl.BlockSpec(memory_space=pltpu.VMEM)
    flops = 2 * n * tiles * length * 128 * 4096
    return pl.pallas_call(
        functools.partial(score_kernel, tiles=tiles, length=length, group=group),
        in_specs=[pl.BlockSpec(memory_space=pltpu.SMEM)] + [vm] * (2 + n),
        out_specs=vm,
        out_shape=jax.ShapeDtypeStruct((n, 4, 128), jnp.float32),
        scratch_shapes=[pltpu.VMEM((n, 8, 128), jnp.float32)],
        compiler_params=pltpu.CompilerParams(vmem_limit_bytes=32 << 20),
        cost_estimate=pl.CostEstimate(flops=2 * flops, bytes_accessed=0, transcendentals=0),
        name=f"score_{n}",
    )(place, mine, other, *parcels)


def shards(tokens, w_in, b_in, w_out, b_out, gain, shift, proj, tiles, lengths, slots, counts):
    queries, query_len, width = tokens.shape
    count, length, dims = tiles.shape
    half = count // CORES
    core, x, z = lax.axis_index("core"), lax.axis_index("x"), lax.axis_index("z")

    valid = jnp.arange(4, dtype=jnp.int32)[None, :] < counts
    codes = jnp.where(valid, slots[:, 0, :], count).astype(jnp.bfloat16)
    codes = codes.reshape(X, Z, queries, 4).transpose(3, 1, 0, 2).reshape(4 * Z, X * queries)
    codes_far = lax.ppermute(codes, "core", turn(CORES, 1))
    low, high = jnp.where(core == 0, codes, codes_far), jnp.where(core == 0, codes_far, codes)
    both = jnp.concatenate([low, high], axis=1)

    part = lax.dynamic_slice(tiles, (core * half, 0, 0), (half, length, dims))
    sizes = lax.dynamic_slice(lengths, (core * half,), (half,))
    real = jnp.arange(length, dtype=jnp.int32)[None, :] < sizes[:, None]
    part = jnp.where(real[:, :, None], part, part[:, 0:1, :])
    own = jnp.concatenate([part.reshape(half * length, dims), both], axis=0)

    up, down = [own], [own]
    for _ in range(3):
        up.append(lax.ppermute(up[-1], "z", turn(Z, 1)))
        down.append(lax.ppermute(down[-1], "z", turn(Z, -1)))
    up.append(lax.ppermute(up[-1], "z", turn(Z, 1)))

    flat = tokens.reshape(queries * query_len, width)
    begun, finish = encode(
        flat, w_in, b_in[None], w_out, b_out[None], gain[None], shift[None], proj, queries, query_len
    )
    embeds = finish(begun)
    near = [embeds] + [lax.ppermute(embeds, "x", turn(X, k)) for k in (1, -1, 2)]
    mine = jnp.concatenate(near, axis=0)
    other = lax.ppermute(mine, "core", turn(CORES, 1))

    xs = jnp.stack([x, (x - 1) % X, (x + 1) % X, (x + 2) % X])
    place = jnp.concatenate([core * X + xs, (1 - core) * X + xs, jnp.stack([z, core * half])]).astype(jnp.int32)
    args = (half, length, queries)
    part_a = score(place, mine, other, [own, up[1], down[1], up[2], down[2]], *args)
    part_b = score(place, mine, other, [up[3], down[3]], *args)
    part_c = score(place, mine, other, [up[4]], *args)
    ring = [part_a[0], part_a[2], part_a[4], part_b[1], part_c[0], part_b[0], part_a[3], part_a[1]]
    ring = jnp.stack(ring + ring)
    found = lax.dynamic_slice(ring, (Z - z, 0, 0), (Z, 4, 128))
    found = found.reshape(Z, 4, CORES, X * queries)
    give = jnp.where(core == 0, found[:, :, 1], found[:, :, 0])
    keep = jnp.where(core == 0, found[:, :, 0], found[:, :, 1])
    summed = keep + lax.ppermute(give, "core", turn(CORES, 1))
    summed = summed.reshape(Z, 4, X, queries).transpose(2, 0, 1, 3)
    summed = lax.all_to_all(summed, "x", split_axis=0, concat_axis=0, tiled=True)
    return summed.transpose(3, 0, 1, 2).reshape(queries, X * Z, 4)


def solution(mesh):
    fine = Mesh(mesh.devices.reshape(Y, CORES, X, Z), ("y", "core", "x", "z"))
    group, shard = ("y", "core"), ("x", "z")
    placed = (P(group + shard),) + (P(),) * 7 + (P(shard), P(shard), P(group, shard), P(group, shard))
    return jax.shard_map(shards, mesh=fine, in_specs=placed, out_specs=P(group + shard), check_vma=False)
```

```python
import functools

import jax
import jax.numpy as jnp
from jax import lax
from jax.experimental import pallas as pl
from jax.experimental.pallas import tpu as pltpu
from jax.sharding import Mesh
from jax.sharding import PartitionSpec as P

Y, CORES, X, Z = 4, 2, 4, 8
HALF_ROOT = 0.7071067811865476


def turn(size, step):
    return [(i, (i + step) % size) for i in range(size)]


def gelu(pre):
    return 0.5 * pre * (1.0 + lax.erf(pre * jnp.float32(HALF_ROOT)))


def ffn_kernel(tok, w_in, b_in, w_out, b_out, gain, shift, proj, out, acc, turned, *, queries, tokens):
    step = pl.program_id(0)
    pre = jnp.dot(tok[...], w_in[...], preferred_element_type=jnp.float32) + b_in[...]
    hidden = gelu(pre).astype(jnp.bfloat16)
    part = jnp.dot(hidden, w_out[...], preferred_element_type=jnp.float32)

    @pl.when(step == 0)
    def _():
        acc[...] = part

    @pl.when(step > 0)
    def _():
        acc[...] += part

    @pl.when(step == pl.num_programs(0) - 1)
    def _():
        total = acc[...] + b_out[...] + tok[...].astype(jnp.float32)
        diff = total - jnp.mean(total, axis=-1, keepdims=True)
        spread = jnp.mean(diff * diff, axis=-1, keepdims=True)
        normed = (diff * lax.rsqrt(spread + 1e-5) * gain[...] + shift[...]).astype(jnp.bfloat16)
        projected = jnp.dot(normed, proj[...], preferred_element_type=jnp.float32)
        scale = lax.rsqrt(jnp.sum(projected * projected, axis=-1, keepdims=True) + 1e-6)
        embeds = projected * scale
        for q in range(queries):
            turned[pl.ds(q, tokens, stride=queries), :] = embeds[q * tokens : (q + 1) * tokens, :]
        out[...] = turned[...].astype(jnp.bfloat16)


def encode(tok, w_in, b_in, w_out, b_out, gain, shift, proj, queries, tokens, chunk=1024):
    rows, width = tok.shape

    def whole(a):
        return pl.BlockSpec(a.shape, lambda j: (0,) * a.ndim)

    return pl.pallas_call(
        functools.partial(ffn_kernel, queries=queries, tokens=tokens),
        grid=(w_in.shape[1] // chunk,),
        in_specs=[
            whole(tok),
            pl.BlockSpec((width, chunk), lambda j: (0, j)),
            pl.BlockSpec((1, chunk), lambda j: (0, j)),
            pl.BlockSpec((chunk, width), lambda j: (j, 0)),
            whole(b_out),
            whole(gain),
            whole(shift),
            whole(proj),
        ],
        out_specs=pl.BlockSpec((rows, proj.shape[1]), lambda j: (0, 0)),
        out_shape=jax.ShapeDtypeStruct((rows, proj.shape[1]), jnp.bfloat16),
        scratch_shapes=[pltpu.VMEM((rows, width), jnp.float32), pltpu.VMEM((rows, proj.shape[1]), jnp.float32)],
        compiler_params=pltpu.CompilerParams(vmem_limit_bytes=60 << 20),
        cost_estimate=pl.CostEstimate(flops=8 * rows * w_in.size, bytes_accessed=4 * w_in.size, transcendentals=0),
        name="encode",
    )(tok, w_in, b_in, w_out, b_out, gain, shift, proj)


def parcel_kernel(place, sizes, near, far, tiles, out):
    half, length, _ = tiles.shape
    column = lax.broadcasted_iota(jnp.int32, tiles.shape[1:], 0)
    for t in range(half):
        tile = tiles[t].astype(jnp.float32)
        size = sizes[place[0] * half + t]
        out[t * length : (t + 1) * length, :] = jnp.where(column < size, tile, tile[0:1, :]).astype(jnp.bfloat16)
    for source, core in ((near, place[0]), (far, 1 - place[0])):
        codes = source[...]
        blank = jnp.zeros((4, 128), jnp.float32)
        lines = []
        for x in range(X):
            lines += [codes[:, x * 128 : (x + 1) * 128], blank]
        start = pl.multiple_of(half * length + core * (8 * X), 8 * X)
        out[pl.ds(start, 8 * X), :] = jnp.concatenate(lines, axis=0).astype(jnp.bfloat16)


def make_parcel(place, sizes, near, far, tiles):
    count, length, dims = tiles.shape
    half = count // CORES
    rows = half * length + 8 * X * CORES
    return pl.pallas_call(
        parcel_kernel,
        grid_spec=pltpu.PrefetchScalarGridSpec(
            num_scalar_prefetch=2,
            grid=(1,),
            in_specs=[
                pl.BlockSpec(near.shape, lambda i, *_: (0, 0)),
                pl.BlockSpec(far.shape, lambda i, *_: (0, 0)),
                pl.BlockSpec((half, length, dims), lambda i, place, sizes: (place[0], 0, 0)),
            ],
            out_specs=pl.BlockSpec((rows, dims), lambda i, *_: (0, 0)),
        ),
        out_shape=jax.ShapeDtypeStruct((rows, dims), jnp.bfloat16),
        name="parcel",
    )(place, sizes, near, far, tiles)


def score_kernel(place, mine, other, *refs, tiles, length, group, steps, shards, chained):
    parcels, out, acc = refs[: len(shards)], refs[-2], refs[-1]
    rows = tiles * length
    lane_group = lax.broadcasted_iota(jnp.int32, (8, 128), 1) // group
    row = lax.broadcasted_iota(jnp.int32, (8, 128), 0)
    core, x, z = place[0], place[1], place[2]

    def one(step, _):
        for side, queries in enumerate((mine, other)):
            start = pl.multiple_of(step * 512, 512)
            block = queries[pl.ds(start, 512), :]
            source = lax.rem(x + place[4 + step], X)
            here = lane_group == source + X * (core if side == 0 else 1 - core)
            for n, parcel in enumerate(parcels):
                similar = lax.dot_general(
                    parcel[0:rows, :], block, (((1,), (1,)), ((), ())), preferred_element_type=jnp.float32
                )
                sums = []
                for t in range(tiles):
                    best = jnp.max(similar[t * length : (t + 1) * length], axis=0, keepdims=True)
                    sums.append(best[:, 0:128] + best[:, 128:256] + best[:, 256:384] + best[:, 384:512])
                sums = jnp.concatenate(sums + [jnp.zeros((8 - tiles, 128), jnp.float32)], axis=0)
                sums = sums + pltpu.roll(sums, 64, 1)
                sums = sums + pltpu.roll(sums, 32, 1)
                sums = sums + pltpu.roll(sums, 16, 1)
                acc[n] = jnp.where(here, sums, acc[n])
        return 0

    lax.fori_loop(0, 4, one, 0, unroll=steps)
    first_tile = core * tiles
    if chained:
        out[...] = refs[len(shards)][...]
    for n, parcel in enumerate(parcels):
        codes = parcel[rows : rows + 8 * X * CORES, :].astype(jnp.float32)
        code = jnp.zeros((8, 128), jnp.float32)
        for d in range(X * CORES):
            turned = pltpu.roll(codes[d * 8 : d * 8 + 8], lax.rem((d - z) * group + 128, 128), 1)
            code = jnp.where(lane_group == d, turned, code)
        code = code.astype(jnp.int32) - first_tile
        shard = lax.rem(z + shards[n], Z)
        for c in range(4):
            picked = (code[c : c + 1] == row) & (row < tiles)
            line = jnp.sum(jnp.where(picked, acc[n], 0.0), axis=0, keepdims=True)
            out[pl.ds(c * Z + shard, 1), :] = line


def score(place, mine, other, parcels, shards, tiles, length, group, begun=None, steps=1):
    n = len(parcels)
    vm = pl.BlockSpec(memory_space=pltpu.VMEM)
    more = [] if begun is None else [begun]
    return pl.pallas_call(
        functools.partial(
            score_kernel,
            tiles=tiles,
            length=length,
            group=group,
            steps=steps,
            shards=shards,
            chained=begun is not None,
        ),
        in_specs=[pl.BlockSpec(memory_space=pltpu.SMEM)] + [vm] * (2 + n + len(more)),
        out_specs=vm,
        out_shape=jax.ShapeDtypeStruct((4 * Z, 128), jnp.float32),
        scratch_shapes=[pltpu.VMEM((n, 8, 128), jnp.float32)],
        compiler_params=pltpu.CompilerParams(vmem_limit_bytes=32 << 20),
        cost_estimate=pl.CostEstimate(flops=2 * n * tiles * length * 128 * 4096, bytes_accessed=0, transcendentals=0),
        name=f"score_{n}",
    )(place, mine, other, *parcels, *more)


def finish_kernel(place, *refs, group):
    sources, out, table = refs[:4], refs[4], refs[5]
    core, x = place[0], place[1]
    for k, source in enumerate(sources):
        lines = pltpu.roll(source[...], lax.rem(128 - (core * X + x) * group, 128), 1)
        shard = lax.rem(x + place[4 + k], X) * Z
        for c in range(4):
            table[pl.ds(pl.multiple_of(c * X * Z + shard, Z), Z), :] = lines[c * Z : (c + 1) * Z]
    turned = table[...].T
    for c in range(4):
        out[:, c, :] = turned[0:group, c * X * Z : (c + 1) * X * Z]


def finish(place, sources, group):
    vm = pl.BlockSpec(memory_space=pltpu.VMEM)
    return pl.pallas_call(
        functools.partial(finish_kernel, group=group),
        in_specs=[pl.BlockSpec(memory_space=pltpu.SMEM)] + [vm] * 4,
        out_specs=vm,
        out_shape=jax.ShapeDtypeStruct((group, 4, X * Z), jnp.float32),
        scratch_shapes=[pltpu.VMEM((128, 128), jnp.float32)],
        name="finish",
    )(place, *sources)


def shards(tokens, w_in, b_in, w_out, b_out, gain, shift, proj, tiles, lengths, slots, counts):
    queries, query_len, width = tokens.shape
    count, length, dims = tiles.shape
    half = count // CORES
    core, x, z = lax.axis_index("core"), lax.axis_index("x"), lax.axis_index("z")
    place = jnp.stack([core, x, z, 0, 0, X - 1, 1, 2]).astype(jnp.int32)

    wanted = slots.transpose(1, 2, 0)[0]
    valid = jnp.arange(4, dtype=jnp.int32)[:, None] < counts.transpose(1, 0)
    codes = jnp.where(valid, wanted, count).astype(jnp.float32)
    codes_far = lax.ppermute(codes, "core", turn(CORES, 1))
    own = make_parcel(place, lengths, codes, codes_far, tiles)

    def along(a, k):
        return lax.ppermute(a, "z", turn(Z, k))

    up1, down1, up2, down2 = along(own, 1), along(own, -1), along(own, 2), along(own, -2)
    flat, _ = lax.optimization_barrier((tokens.reshape(queries * query_len, width), own))
    embeds = encode(flat, w_in, b_in[None], w_out, b_out[None], gain[None], shift[None], proj, queries, query_len)
    embeds, up1, down1, up2, down2 = lax.optimization_barrier((embeds, up1, down1, up2, down2))
    up3, down3, up4 = along(up2, 1), along(down2, -1), along(up2, 2)

    near = [embeds] + [lax.ppermute(embeds, "x", turn(X, k)) for k in (1, -1, 2)]
    mine = jnp.concatenate(near, axis=0)
    other = lax.ppermute(mine, "core", turn(CORES, 1))

    args = (half, length, queries)
    found = score(place, mine, other, [own, up1, down1, up2, down2], [0, 7, 1, 6, 2], *args)
    found = score(place, mine, other, [up3, down3, up4], [5, 3, 4], *args, begun=found)
    found = found + lax.ppermute(found, "core", turn(CORES, 1))
    sources = [found] + [lax.ppermute(found, "x", turn(X, k)) for k in (1, -1, 2)]
    return finish(place, sources, queries).transpose(0, 2, 1)


def solution(mesh):
    fine = Mesh(mesh.devices.reshape(Y, CORES, X, Z), ("y", "core", "x", "z"))
    group, shard = ("y", "core"), ("x", "z")
    placed = (P(group + shard),) + (P(),) * 7 + (P(shard), P(shard), P(group, shard), P(group, shard))
    return jax.shard_map(shards, mesh=fine, in_specs=placed, out_specs=P(group + shard), check_vma=False)
```

```python
import functools

import jax
import jax.numpy as jnp
from jax import lax
from jax.experimental import pallas as pl
from jax.experimental.pallas import tpu as pltpu
from jax.sharding import Mesh
from jax.sharding import PartitionSpec as P

Y, CORES, X, Z = 4, 2, 4, 8
HALF_ROOT = 0.7071067811865476


def turn(size, step):
    return [(i, (i + step) % size) for i in range(size)]


def gelu(pre):
    return 0.5 * pre * (1.0 + lax.erf(pre * jnp.float32(HALF_ROOT)))


def ffn_part(tok, w_in, b_in, w_out, skip):
    chunk = w_in.shape[1]
    start = pl.multiple_of((pl.program_id(0) + skip) * chunk, chunk)
    pre = jnp.dot(tok[...], w_in[...], preferred_element_type=jnp.float32) + b_in[pl.ds(start, chunk)][None, :]
    hidden = gelu(pre).astype(jnp.bfloat16)
    return jnp.dot(hidden, w_out[...], preferred_element_type=jnp.float32)


def encode_first(tok, w_in, b_in, w_out, acc):
    part = ffn_part(tok, w_in, b_in, w_out, 0)

    @pl.when(pl.program_id(0) == 0)
    def _():
        acc[...] = part

    @pl.when(pl.program_id(0) > 0)
    def _():
        acc[...] += part


def encode_second(tok, w_in, b_in, w_out, begun, b_out, gain, shift, proj, out, acc, turned, *, queries, tokens, skip):
    step = pl.program_id(0)
    part = ffn_part(tok, w_in, b_in, w_out, skip)

    @pl.when(step == 0)
    def _():
        acc[...] = begun[...] + part

    @pl.when(step > 0)
    def _():
        acc[...] += part

    @pl.when(step == pl.num_programs(0) - 1)
    def _():
        total = acc[...] + b_out[...][None, :] + tok[...].astype(jnp.float32)
        diff = total - jnp.mean(total, axis=-1, keepdims=True)
        spread = jnp.mean(diff * diff, axis=-1, keepdims=True)
        normed = diff * lax.rsqrt(spread + 1e-5) * gain[...][None, :] + shift[...][None, :]
        projected = jnp.dot(normed.astype(jnp.bfloat16), proj[...], preferred_element_type=jnp.float32)
        scale = lax.rsqrt(jnp.sum(projected * projected, axis=-1, keepdims=True) + 1e-6)
        embeds = projected * scale
        for q in range(queries):
            turned[pl.ds(q, tokens, stride=queries), :] = embeds[q * tokens : (q + 1) * tokens, :]
        out[...] = turned[...].astype(jnp.bfloat16)


def whole(a):
    return pl.BlockSpec(a.shape, lambda j: (0,) * a.ndim)


def ffn_specs(tok, w_in, b_in, chunk, skip):
    width = tok.shape[1]
    return [
        whole(tok),
        pl.BlockSpec((width, chunk), lambda j: (0, j + skip)),
        whole(b_in),
        pl.BlockSpec((chunk, width), lambda j: (j + skip, 0)),
    ]


FREE = pl.CostEstimate(flops=1000, bytes_accessed=1000, transcendentals=0)


def encode(tok, w_in, b_in, w_out, chunk=768):
    steps = w_in.shape[1] // chunk // 2
    return pl.pallas_call(
        encode_first,
        grid=(steps,),
        in_specs=ffn_specs(tok, w_in, b_in, chunk, 0),
        out_specs=whole(tok),
        out_shape=jax.ShapeDtypeStruct(tok.shape, jnp.float32),
        compiler_params=pltpu.CompilerParams(vmem_limit_bytes=60 << 20),
        cost_estimate=FREE,
        name="encode_first",
    )(tok, w_in, b_in, w_out)


def encode_rest(tok, w_in, b_in, w_out, begun, b_out, gain, shift, proj, queries, tokens, chunk=768):
    rows, width = tok.shape
    steps = w_in.shape[1] // chunk // 2
    return pl.pallas_call(
        functools.partial(encode_second, queries=queries, tokens=tokens, skip=steps),
        grid=(steps,),
        in_specs=ffn_specs(tok, w_in, b_in, chunk, steps) + [whole(a) for a in (begun, b_out, gain, shift, proj)],
        out_specs=pl.BlockSpec((rows, proj.shape[1]), lambda j: (0, 0)),
        out_shape=jax.ShapeDtypeStruct((rows, proj.shape[1]), jnp.bfloat16),
        scratch_shapes=[pltpu.VMEM((rows, width), jnp.float32), pltpu.VMEM((rows, proj.shape[1]), jnp.float32)],
        compiler_params=pltpu.CompilerParams(vmem_limit_bytes=60 << 20),
        cost_estimate=FREE,
        name="encode_second",
    )(tok, w_in, b_in, w_out, begun, b_out, gain, shift, proj)


def parcel_kernel(sizes, near, far, tiles, out, *, half):
    length = tiles.shape[1]
    core = lax.axis_index("core")
    column = lax.broadcasted_iota(jnp.int32, tiles.shape[1:], 0)
    for t in range(half):
        tile = tiles[core * half + t].astype(jnp.float32)
        size = sizes[core * half + t]
        out[t * length : (t + 1) * length, :] = jnp.where(column < size, tile, tile[0:1, :]).astype(jnp.bfloat16)
    for source, side in ((near, core), (far, 1 - core)):
        codes = source[...]
        blank = jnp.zeros((4, 128), jnp.float32)
        lines = []
        for x in range(X):
            lines += [codes[:, x * 128 : (x + 1) * 128], blank]
        start = pl.multiple_of(half * length + side * (8 * X), 8 * X)
        out[pl.ds(start, 8 * X), :] = jnp.concatenate(lines, axis=0).astype(jnp.bfloat16)


VM = pl.BlockSpec(memory_space=pltpu.VMEM)


def make_parcel(sizes, near, far, tiles):
    count, length, dims = tiles.shape
    half = count // CORES
    return pl.pallas_call(
        functools.partial(parcel_kernel, half=half),
        in_specs=[pl.BlockSpec(memory_space=pltpu.SMEM), VM, VM, VM],
        out_specs=VM,
        out_shape=jax.ShapeDtypeStruct((half * length + 8 * X * CORES, dims), jnp.bfloat16),
        name="parcel",
    )(sizes, near, far, tiles)


SENDER = (0, X - 1, 1, 2)


def score_kernel(*refs, sides, tiles, length, group, shards, chained):
    n, s = len(shards), len(sides)
    blocks, parcels, out, acc = refs[:s], refs[s : s + n], refs[-2], refs[-1]
    rows = tiles * length
    lane_group = lax.broadcasted_iota(jnp.int32, (8, 128), 1) // group
    row = lax.broadcasted_iota(jnp.int32, (8, 128), 0)
    core, x, z = lax.axis_index("core"), lax.axis_index("x"), lax.axis_index("z")
    acc[...] = jnp.zeros_like(acc)

    for step in range(X):
        for side, queries in zip(sides, blocks):
            block = queries[step * 512 : (step + 1) * 512, :]
            source = lax.rem(x + SENDER[step], X)
            here = lane_group == source + X * (core if side == 0 else 1 - core)
            for n, parcel in enumerate(parcels):
                similar = lax.dot_general(
                    parcel[0:rows, :], block, (((1,), (1,)), ((), ())), preferred_element_type=jnp.float32
                )
                sums = []
                for t in range(tiles):
                    best = jnp.max(similar[t * length : (t + 1) * length], axis=0, keepdims=True)
                    sums.append(best[:, 0:128] + best[:, 128:256] + best[:, 256:384] + best[:, 384:512])
                sums = jnp.concatenate(sums + [jnp.zeros((8 - tiles, 128), jnp.float32)], axis=0)
                sums = sums + pltpu.roll(sums, 64, 1)
                sums = sums + pltpu.roll(sums, 32, 1)
                sums = sums + pltpu.roll(sums, 16, 1)
                acc[n] = jnp.where(here, sums, acc[n])

    first_tile = core * tiles
    out[...] = refs[s + len(shards)][...] if chained else jnp.zeros_like(out)
    for n, parcel in enumerate(parcels):
        codes = parcel[rows : rows + 8 * X * CORES, :].astype(jnp.float32)
        code = jnp.zeros((8, 128), jnp.float32)
        for d in range(X * CORES):
            turned = pltpu.roll(codes[d * 8 : d * 8 + 8], lax.rem((d - z) * group + 128, 128), 1)
            code = jnp.where(lane_group == d, turned, code)
        code = code.astype(jnp.int32) - first_tile
        shard = lax.rem(z + shards[n] * (2 * core - 1) + Z, Z)
        for c in range(4):
            picked = (code[c : c + 1] == row) & (row < tiles)
            line = jnp.sum(jnp.where(picked, acc[n], 0.0), axis=0, keepdims=True)
            out[pl.ds(c * Z + shard, 1), :] += line


def score(blocks, parcels, shards, tiles, length, group, begun=None):
    n = len(parcels)
    more = [] if begun is None else [begun]
    return pl.pallas_call(
        functools.partial(
            score_kernel,
            sides=tuple(blocks),
            tiles=tiles,
            length=length,
            group=group,
            shards=shards,
            chained=begun is not None,
        ),
        in_specs=[VM] * (len(blocks) + n + len(more)),
        out_specs=VM,
        out_shape=jax.ShapeDtypeStruct((4 * Z, 128), jnp.float32),
        scratch_shapes=[pltpu.VMEM((n, 8, 128), jnp.float32)],
        compiler_params=pltpu.CompilerParams(vmem_limit_bytes=32 << 20),
        cost_estimate=FREE,
        name=f"score_{len(blocks)}_{n}",
    )(*blocks.values(), *parcels, *more)


def finish_kernel(*refs, group):
    sources, out, table = refs[:4], refs[4], refs[5]
    core, x = lax.axis_index("core"), lax.axis_index("x")
    for sender, source in zip(SENDER, sources):
        lines = pltpu.roll(source[...], lax.rem(128 - (core * X + x) * group, 128), 1)
        shard = lax.rem(x + sender, X) * Z
        for c in range(4):
            table[pl.ds(pl.multiple_of(c * X * Z + shard, Z), Z), :] = lines[c * Z : (c + 1) * Z]
    turned = table[...].T
    for c in range(4):
        out[:, c, :] = turned[0:group, c * X * Z : (c + 1) * X * Z]


def finish(sources, group):
    return pl.pallas_call(
        functools.partial(finish_kernel, group=group),
        in_specs=[VM] * 4,
        out_specs=VM,
        out_shape=jax.ShapeDtypeStruct((group, 4, X * Z), jnp.float32),
        scratch_shapes=[pltpu.VMEM((128, 128), jnp.float32)],
        name="finish",
    )(*sources)


def tied(*arrays):
    return lax.optimization_barrier(arrays)


def shards(tokens, w_in, b_in, w_out, b_out, gain, shift, proj, tiles, lengths, slots, counts):
    queries, query_len, width = tokens.shape
    count, length, dims = tiles.shape
    half = count // CORES

    wanted = slots.transpose(1, 2, 0)[0]
    valid = jnp.arange(4, dtype=jnp.int32)[:, None] < counts.transpose(1, 0)
    codes = jnp.where(valid, wanted, count).astype(jnp.float32)
    codes_far = lax.ppermute(codes, "core", turn(CORES, 1))
    own = make_parcel(lengths, codes, codes_far, tiles)

    ways = [(z, (z + 1) % Z) for z in range(Z)] + [(Z + z, Z + (z - 1) % Z) for z in range(Z)]

    def along(a):
        return lax.ppermute(a, ("core", "z"), ways)

    def across(a, k):
        return lax.ppermute(a, "x", turn(X, k))

    first = along(own)
    flat, _ = tied(tokens.reshape(queries * query_len, width), own)
    begun = encode(flat, w_in, b_in, w_out)
    first, begun = tied(first, begun)
    second = along(first)
    embeds = encode_rest(flat, w_in, b_in, w_out, begun, b_out, gain, shift, proj, queries, query_len)
    second, embeds = tied(second, embeds)
    third = along(second)
    mine = jnp.concatenate([embeds] + [across(embeds, k) for k in (1, -1, 2)], axis=0)
    third, mine = tied(third, mine)
    other = lax.ppermute(mine, "core", turn(CORES, 1))
    fourth = along(third)
    args = (half, length, queries)
    found = score({0: mine}, [own, first, second], (0, 1, 2), *args)
    fourth, found = tied(fourth, found)
    fifth = along(fourth)
    found = score({1: other}, [own, first, second], (0, 1, 2), *args, begun=found)
    fifth, found = tied(fifth, found)
    sixth = along(fifth)
    both = {0: mine, 1: other}
    found = score(both, [third, fourth], (3, 4), *args, begun=found)
    sixth, found = tied(sixth, found)
    seventh = along(sixth)
    found = score(both, [fifth, sixth], (5, 6), *args, begun=found)
    found = score(both, [seventh], (7,), *args, begun=found)
    found = found + lax.ppermute(found, "core", turn(CORES, 1))
    sources = [found] + [across(found, k) for k in (1, -1, 2)]
    return finish(sources, queries).transpose(0, 2, 1)


def solution(mesh):
    fine = Mesh(mesh.devices.reshape(Y, CORES, X, Z), ("y", "core", "x", "z"))
    group, shard = ("y", "core"), ("x", "z")
    placed = (P(group + shard),) + (P(),) * 7 + (P(shard), P(shard), P(group, shard), P(group, shard))
    return jax.shard_map(shards, mesh=fine, in_specs=placed, out_specs=P(group + shard), check_vma=False)
```

```python
import functools

import jax
import jax.numpy as jnp
from jax import lax
from jax.experimental import pallas as pl
from jax.experimental.pallas import tpu as pltpu
from jax.sharding import Mesh
from jax.sharding import PartitionSpec as P

Y, CORES, X, Z = 4, 2, 4, 8
HALF_ROOT = 0.7071067811865476


def turn(size, step):
    return [(i, (i + step) % size) for i in range(size)]


def gelu(pre):
    return 0.5 * pre * (1.0 + lax.erf(pre * jnp.float32(HALF_ROOT)))


FREE = pl.CostEstimate(flops=1000, bytes_accessed=1000, transcendentals=0)


def ffn_kernel(tok, w_in, b_in, w_out, b_out, gain, shift, proj, out, acc, turned, *, queries, tokens):
    step = pl.program_id(0)
    chunk = w_in.shape[1]
    start = pl.multiple_of(step * chunk, chunk)
    pre = jnp.dot(tok[...], w_in[...], preferred_element_type=jnp.float32) + b_in[pl.ds(start, chunk)][None, :]
    hidden = gelu(pre).astype(jnp.bfloat16)
    part = jnp.dot(hidden, w_out[...], preferred_element_type=jnp.float32)

    @pl.when(step == 0)
    def _():
        acc[...] = part

    @pl.when(step > 0)
    def _():
        acc[...] += part

    @pl.when(step == pl.num_programs(0) - 1)
    def _():
        total = acc[...] + b_out[...][None, :] + tok[...].astype(jnp.float32)
        diff = total - jnp.mean(total, axis=-1, keepdims=True)
        spread = jnp.mean(diff * diff, axis=-1, keepdims=True)
        normed = (diff * lax.rsqrt(spread + 1e-5) * gain[...][None, :] + shift[...][None, :]).astype(jnp.bfloat16)
        projected = jnp.dot(normed, proj[...], preferred_element_type=jnp.float32)
        scale = lax.rsqrt(jnp.sum(projected * projected, axis=-1, keepdims=True) + 1e-6)
        embeds = projected * scale
        for q in range(queries):
            turned[pl.ds(q, tokens, stride=queries), :] = embeds[q * tokens : (q + 1) * tokens, :]
        out[...] = turned[...].astype(jnp.bfloat16)


def encode(tok, w_in, b_in, w_out, b_out, gain, shift, proj, queries, tokens, chunk=1024):
    rows, width = tok.shape

    def whole(a):
        return pl.BlockSpec(a.shape, lambda j: (0,) * a.ndim)

    return pl.pallas_call(
        functools.partial(ffn_kernel, queries=queries, tokens=tokens),
        grid=(w_in.shape[1] // chunk,),
        in_specs=[
            whole(tok),
            pl.BlockSpec((width, chunk), lambda j: (0, j)),
            whole(b_in),
            pl.BlockSpec((chunk, width), lambda j: (j, 0)),
            whole(b_out),
            whole(gain),
            whole(shift),
            whole(proj),
        ],
        out_specs=pl.BlockSpec((rows, proj.shape[1]), lambda j: (0, 0)),
        out_shape=jax.ShapeDtypeStruct((rows, proj.shape[1]), jnp.bfloat16),
        scratch_shapes=[pltpu.VMEM((rows, width), jnp.float32), pltpu.VMEM((rows, proj.shape[1]), jnp.float32)],
        compiler_params=pltpu.CompilerParams(vmem_limit_bytes=60 << 20),
        cost_estimate=FREE,
        name="encode",
    )(tok, w_in, b_in, w_out, b_out, gain, shift, proj)


def parcel_kernel(sizes, near, far, tiles, out, *, half):
    length = tiles.shape[1]
    core = lax.axis_index("core")
    column = lax.broadcasted_iota(jnp.int32, tiles.shape[1:], 0)
    for t in range(half):
        tile = tiles[core * half + t].astype(jnp.float32)
        size = sizes[core * half + t]
        out[t * length : (t + 1) * length, :] = jnp.where(column < size, tile, tile[0:1, :]).astype(jnp.bfloat16)
    for source, side in ((near, core), (far, 1 - core)):
        codes = source[...]
        blank = jnp.zeros((4, 128), jnp.float32)
        lines = []
        for x in range(X):
            lines += [codes[:, x * 128 : (x + 1) * 128], blank]
        start = pl.multiple_of(half * length + side * (8 * X), 8 * X)
        out[pl.ds(start, 8 * X), :] = jnp.concatenate(lines, axis=0).astype(jnp.bfloat16)


VM = pl.BlockSpec(memory_space=pltpu.VMEM)


def make_parcel(sizes, near, far, tiles):
    count, length, dims = tiles.shape
    half = count // CORES
    return pl.pallas_call(
        functools.partial(parcel_kernel, half=half),
        in_specs=[pl.BlockSpec(memory_space=pltpu.SMEM), VM, VM, VM],
        out_specs=VM,
        out_shape=jax.ShapeDtypeStruct((half * length + 8 * X * CORES, dims), jnp.bfloat16),
        name="parcel",
    )(sizes, near, far, tiles)


SENDER = (0, X - 1, 1, 2)


def score_kernel(*refs, sides, tiles, length, group, shards, chained):
    n, s = len(shards), len(sides)
    blocks, parcels, out, acc = refs[:s], refs[s : s + n], refs[-2], refs[-1]
    rows = tiles * length
    lane_group = lax.broadcasted_iota(jnp.int32, (8, 128), 1) // group
    row = lax.broadcasted_iota(jnp.int32, (8, 128), 0)
    core, x, z = lax.axis_index("core"), lax.axis_index("x"), lax.axis_index("z")
    acc[...] = jnp.zeros_like(acc)

    for (side, step), queries in zip(sides, blocks):
        block = queries[...]
        source = lax.rem(x + SENDER[step], X)
        here = lane_group == source + X * (core if side == 0 else 1 - core)
        for n, parcel in enumerate(parcels):
            similar = lax.dot_general(
                parcel[0:rows, :], block, (((1,), (1,)), ((), ())), preferred_element_type=jnp.float32
            )
            sums = []
            for t in range(tiles):
                best = jnp.max(similar[t * length : (t + 1) * length], axis=0, keepdims=True)
                sums.append(best[:, 0:128] + best[:, 128:256] + best[:, 256:384] + best[:, 384:512])
            sums = jnp.concatenate(sums + [jnp.zeros((8 - tiles, 128), jnp.float32)], axis=0)
            sums = sums + pltpu.roll(sums, 64, 1)
            sums = sums + pltpu.roll(sums, 32, 1)
            sums = sums + pltpu.roll(sums, 16, 1)
            acc[n] = jnp.where(here, sums, acc[n])

    first_tile = core * tiles
    out[...] = refs[s + len(shards)][...] if chained else jnp.zeros_like(out)
    for n, parcel in enumerate(parcels):
        codes = parcel[rows : rows + 8 * X * CORES, :].astype(jnp.float32)
        code = jnp.zeros((8, 128), jnp.float32)
        for d in range(X * CORES):
            turned = pltpu.roll(codes[d * 8 : d * 8 + 8], lax.rem((d - z) * group + 128, 128), 1)
            code = jnp.where(lane_group == d, turned, code)
        code = code.astype(jnp.int32) - first_tile
        shard = lax.rem(z + shards[n] * (2 * core - 1) + Z, Z)
        for c in range(4):
            picked = (code[c : c + 1] == row) & (row < tiles)
            line = jnp.sum(jnp.where(picked, acc[n], 0.0), axis=0, keepdims=True)
            out[pl.ds(c * Z + shard, 1), :] += line


def score(blocks, parcels, shards, tiles, length, group, begun=None):
    n = len(parcels)
    more = [] if begun is None else [begun]
    return pl.pallas_call(
        functools.partial(
            score_kernel,
            sides=tuple(blocks),
            tiles=tiles,
            length=length,
            group=group,
            shards=shards,
            chained=begun is not None,
        ),
        in_specs=[VM] * (len(blocks) + n + len(more)),
        out_specs=VM,
        out_shape=jax.ShapeDtypeStruct((4 * Z, 128), jnp.float32),
        scratch_shapes=[pltpu.VMEM((n, 8, 128), jnp.float32)],
        compiler_params=pltpu.CompilerParams(vmem_limit_bytes=32 << 20),
        cost_estimate=FREE,
        name=f"score_{len(blocks)}_{n}",
    )(*blocks.values(), *parcels, *more)


def finish_kernel(*refs, group):
    sources, out, table = refs[:4], refs[4], refs[5]
    core, x = lax.axis_index("core"), lax.axis_index("x")
    for sender, source in zip(SENDER, sources):
        lines = pltpu.roll(source[...], lax.rem(128 - (core * X + x) * group, 128), 1)
        shard = lax.rem(x + sender, X) * Z
        for c in range(4):
            table[pl.ds(pl.multiple_of(c * X * Z + shard, Z), Z), :] = lines[c * Z : (c + 1) * Z]
    turned = table[...].T
    for c in range(4):
        out[:, c, :] = turned[0:group, c * X * Z : (c + 1) * X * Z]


def finish(sources, group):
    return pl.pallas_call(
        functools.partial(finish_kernel, group=group),
        in_specs=[VM] * 4,
        out_specs=VM,
        out_shape=jax.ShapeDtypeStruct((group, 4, X * Z), jnp.float32),
        scratch_shapes=[pltpu.VMEM((128, 128), jnp.float32)],
        name="finish",
    )(*sources)


def tied(*arrays):
    return lax.optimization_barrier(arrays)


def shards(tokens, w_in, b_in, w_out, b_out, gain, shift, proj, tiles, lengths, slots, counts):
    queries, query_len, width = tokens.shape
    count, length, dims = tiles.shape
    half = count // CORES

    wanted = slots.transpose(1, 2, 0)[0]
    valid = jnp.arange(4, dtype=jnp.int32)[:, None] < counts.transpose(1, 0)
    codes = jnp.where(valid, wanted, count).astype(jnp.float32)
    codes_far = lax.ppermute(codes, "core", turn(CORES, 1))
    own = make_parcel(lengths, codes, codes_far, tiles)

    def along(a, k):
        ways = [(z, (z + k) % Z) for z in range(Z)] + [(Z + z, Z + (z - k) % Z) for z in range(Z)]
        return lax.ppermute(a, ("core", "z"), ways)

    def across(a, k):
        return lax.ppermute(a, "x", turn(X, k))

    def swap(a):
        return lax.ppermute(a, "core", turn(CORES, 1))

    near = {k: along(own, k) for k in (1, -1, 2, -2)}
    flat, _ = tied(tokens.reshape(queries * query_len, width), own)
    embeds = encode(flat, w_in, b_in, w_out, b_out, gain, shift, proj, queries, query_len)
    near[1], near[-1], near[2], near[-2], embeds = tied(near[1], near[-1], near[2], near[-2], embeds)
    near[3], near[-3], near[4] = along(near[2], 1), along(near[-2], -1), along(near[2], 2)
    mine = [embeds] + [across(embeds, k) for k in (1, -1, 2)]
    other = [swap(embeds)]
    args = (half, length, queries)
    early = ([own, near[1], near[-1], near[2], near[-2]], (0, 1, -1, 2, -2))
    found = score({(0, 0): embeds, (1, 0): other[0]}, *early, *args)
    found, mine[1], mine[2], mine[3] = tied(found, mine[1], mine[2], mine[3])
    other += [swap(a) for a in mine[1:]]
    found = score({(0, k): mine[k] for k in (1, 2, 3)}, *early, *args, begun=found)
    found, near[3], near[-3], near[4] = tied(found, near[3], near[-3], near[4])
    found = score({(1, k): other[k] for k in (1, 2, 3)}, *early, *args, begun=found)
    every = {(0, k): mine[k] for k in range(4)} | {(1, k): other[k] for k in range(4)}
    found = score(every, [near[3], near[-3], near[4]], (3, -3, 4), *args, begun=found)
    found = found + swap(found)
    sources = [found] + [across(found, k) for k in (1, -1, 2)]
    return finish(sources, queries).transpose(0, 2, 1)


def solution(mesh):
    fine = Mesh(mesh.devices.reshape(Y, CORES, X, Z), ("y", "core", "x", "z"))
    group, shard = ("y", "core"), ("x", "z")
    placed = (P(group + shard),) + (P(),) * 7 + (P(shard), P(shard), P(group, shard), P(group, shard))
    return jax.shard_map(shards, mesh=fine, in_specs=placed, out_specs=P(group + shard), check_vma=False)
```

```python
import functools

import jax
import jax.numpy as jnp
from jax import lax
from jax.experimental import pallas as pl
from jax.experimental.pallas import tpu as pltpu
from jax.sharding import Mesh
from jax.sharding import PartitionSpec as P

Y, CORES, X, Z = 4, 2, 4, 8
HALF_ROOT = 0.7071067811865476


def turn(size, step):
    return [(i, (i + step) % size) for i in range(size)]


def gelu(pre):
    return 0.5 * pre * (1.0 + lax.erf(pre * jnp.float32(HALF_ROOT)))


FREE = pl.CostEstimate(flops=1000, bytes_accessed=1000, transcendentals=0)


def ffn_kernel(tok, w_in, b_in, w_out, b_out, gain, shift, proj, out, again, acc, turned, *, queries, tokens):
    step = pl.program_id(0)
    chunk = w_in.shape[1]
    start = pl.multiple_of(step * chunk, chunk)
    pre = jnp.dot(tok[...], w_in[...], preferred_element_type=jnp.float32) + b_in[pl.ds(start, chunk)][None, :]
    hidden = gelu(pre).astype(jnp.bfloat16)
    part = jnp.dot(hidden, w_out[...], preferred_element_type=jnp.float32)

    @pl.when(step == 0)
    def _():
        acc[...] = part

    @pl.when(step > 0)
    def _():
        acc[...] += part

    @pl.when(step == pl.num_programs(0) - 1)
    def _():
        total = acc[...] + b_out[...][None, :] + tok[...].astype(jnp.float32)
        diff = total - jnp.mean(total, axis=-1, keepdims=True)
        spread = jnp.mean(diff * diff, axis=-1, keepdims=True)
        normed = (diff * lax.rsqrt(spread + 1e-5) * gain[...][None, :] + shift[...][None, :]).astype(jnp.bfloat16)
        projected = jnp.dot(normed, proj[...], preferred_element_type=jnp.float32)
        scale = lax.rsqrt(jnp.sum(projected * projected, axis=-1, keepdims=True) + 1e-6)
        embeds = projected * scale
        for q in range(queries):
            turned[pl.ds(q, tokens, stride=queries), :] = embeds[q * tokens : (q + 1) * tokens, :]
        out[...] = turned[...].astype(jnp.bfloat16)
        again[...] = turned[...].astype(jnp.bfloat16)


def encode(tok, w_in, b_in, w_out, b_out, gain, shift, proj, queries, tokens, chunk=1024):
    rows, width = tok.shape

    def whole(a):
        return pl.BlockSpec(a.shape, lambda j: (0,) * a.ndim)

    return pl.pallas_call(
        functools.partial(ffn_kernel, queries=queries, tokens=tokens),
        grid=(w_in.shape[1] // chunk,),
        in_specs=[
            whole(tok),
            pl.BlockSpec((width, chunk), lambda j: (0, j)),
            whole(b_in),
            pl.BlockSpec((chunk, width), lambda j: (j, 0)),
            whole(b_out),
            whole(gain),
            whole(shift),
            whole(proj),
        ],
        out_specs=[pl.BlockSpec((rows, proj.shape[1]), lambda j: (0, 0))] * 2,
        out_shape=[jax.ShapeDtypeStruct((rows, proj.shape[1]), jnp.bfloat16)] * 2,
        scratch_shapes=[pltpu.VMEM((rows, width), jnp.float32), pltpu.VMEM((rows, proj.shape[1]), jnp.float32)],
        compiler_params=pltpu.CompilerParams(vmem_limit_bytes=60 << 20),
        cost_estimate=FREE,
        name="encode",
    )(tok, w_in, b_in, w_out, b_out, gain, shift, proj)


def parcel_kernel(sizes, slots, counts, tiles, out, *, half):
    count, length = tiles.shape[:2]
    core = lax.axis_index("core")
    column = lax.broadcasted_iota(jnp.int32, tiles.shape[1:], 0)
    for t in range(half):
        tile = tiles[core * half + t].astype(jnp.float32)
        size = sizes[core * half + t]
        out[t * length : (t + 1) * length, :] = jnp.where(column < size, tile, tile[0:1, :]).astype(jnp.bfloat16)
    order = lax.broadcasted_iota(jnp.int32, slots.shape, 0)
    codes = jnp.where(order < counts[...], slots[...], count).astype(jnp.float32)
    lines = []
    for x in range(X):
        lines += [codes[:, x * 128 : (x + 1) * 128], jnp.zeros((4, 128), jnp.float32)]
    out[half * length : half * length + 8 * X, :] = jnp.concatenate(lines, axis=0).astype(jnp.bfloat16)


VM = pl.BlockSpec(memory_space=pltpu.VMEM)


def make_parcel(sizes, slots, counts, tiles):
    count, length, dims = tiles.shape
    half = count // CORES
    return pl.pallas_call(
        functools.partial(parcel_kernel, half=half),
        in_specs=[pl.BlockSpec(memory_space=pltpu.SMEM), VM, VM, VM],
        out_specs=VM,
        out_shape=jax.ShapeDtypeStruct((half * length + 8 * X, dims), jnp.bfloat16),
        name="parcel",
    )(sizes, slots, counts, tiles)


SENDER = (0, X - 1, 1, 2)


def score_kernel(*refs, senders, items, arrays, tiles, length, group, chained):
    s, n = len(senders), len(items)
    blocks, held, out, acc = refs[:s], refs[s : s + arrays], refs[-2], refs[-1]
    rows = tiles * length
    lane_group = lax.broadcasted_iota(jnp.int32, (8, 128), 1) // group
    row = lax.broadcasted_iota(jnp.int32, (8, 128), 0)
    core, x, z = lax.axis_index("core"), lax.axis_index("x"), lax.axis_index("z")
    acc[...] = jnp.zeros_like(acc)

    for sender, queries in zip(senders, blocks):
        block = queries[...]
        here = lane_group == lax.rem(x + SENDER[sender], X)
        for n, (parcel, *_) in enumerate(items):
            similar = lax.dot_general(
                held[parcel][0:rows, :], block, (((1,), (1,)), ((), ())), preferred_element_type=jnp.float32
            )
            sums = []
            for t in range(tiles):
                best = jnp.max(similar[t * length : (t + 1) * length], axis=0, keepdims=True)
                sums.append(best[:, 0:128] + best[:, 128:256] + best[:, 256:384] + best[:, 384:512])
            sums = jnp.concatenate(sums + [jnp.zeros((8 - tiles, 128), jnp.float32)], axis=0)
            sums = sums + pltpu.roll(sums, 64, 1)
            sums = sums + pltpu.roll(sums, 32, 1)
            sums = sums + pltpu.roll(sums, 16, 1)
            acc[n] = jnp.where(here, sums, acc[n])

    out[...] = refs[s + arrays][...] if chained else jnp.zeros_like(out)
    way = 2 * core - 1
    for n, (_, label, steps, far) in enumerate(items):
        codes = held[label][rows : rows + 8 * X, :].astype(jnp.float32)
        code = jnp.full((8, 128), -1.0, jnp.float32)
        for d in range(X):
            turned = pltpu.roll(codes[d * 8 : d * 8 + 8], lax.rem((d - z) * group + 128, 128), 1)
            code = jnp.where(lane_group == d, turned, code)
        code = code.astype(jnp.int32) - tiles * (1 - core if far else core)
        shard = lax.rem(z + steps * way + Z, Z)
        for c in range(4):
            picked = (code[c : c + 1] == row) & (row < tiles)
            line = jnp.sum(jnp.where(picked, acc[n], 0.0), axis=0, keepdims=True)
            out[pl.ds(c * Z + shard, 1), :] += line


def score(blocks, items, tiles, length, group, begun=None):
    held = []

    def at(array):
        for i, one in enumerate(held):
            if one is array:
                return i
        held.append(array)
        return len(held) - 1

    plan = tuple((at(parcel), at(label), steps, far) for parcel, label, steps, far in items)
    more = [] if begun is None else [begun]
    return pl.pallas_call(
        functools.partial(
            score_kernel,
            senders=tuple(blocks),
            items=plan,
            arrays=len(held),
            tiles=tiles,
            length=length,
            group=group,
            chained=begun is not None,
        ),
        in_specs=[VM] * (len(blocks) + len(held) + len(more)),
        out_specs=VM,
        out_shape=jax.ShapeDtypeStruct((4 * Z, 128), jnp.float32),
        scratch_shapes=[pltpu.VMEM((len(plan), 8, 128), jnp.float32)],
        compiler_params=pltpu.CompilerParams(vmem_limit_bytes=32 << 20),
        cost_estimate=FREE,
        name=f"score_{len(blocks)}_{len(plan)}",
    )(*blocks.values(), *held, *more)


def finish_kernel(*refs, group):
    sources, out, table = refs[:4], refs[4], refs[5]
    x = lax.axis_index("x")
    for sender, source in zip(SENDER, sources):
        lines = pltpu.roll(source[...], lax.rem(128 - x * group, 128), 1)
        shard = lax.rem(x + sender, X) * Z
        for c in range(4):
            table[pl.ds(pl.multiple_of(c * X * Z + shard, Z), Z), :] = lines[c * Z : (c + 1) * Z]
    turned = table[...].T
    for c in range(4):
        out[:, c, :] = turned[0:group, c * X * Z : (c + 1) * X * Z]


def finish(sources, group):
    return pl.pallas_call(
        functools.partial(finish_kernel, group=group),
        in_specs=[VM] * 4,
        out_specs=VM,
        out_shape=jax.ShapeDtypeStruct((group, 4, X * Z), jnp.float32),
        scratch_shapes=[pltpu.VMEM((128, 128), jnp.float32)],
        name="finish",
    )(*sources)


def tied(*arrays):
    return lax.optimization_barrier(arrays)


def shards(tokens, w_in, b_in, w_out, b_out, gain, shift, proj, tiles, lengths, slots, counts):
    queries, query_len, width = tokens.shape
    count, length, dims = tiles.shape
    half = count // CORES
    own = make_parcel(lengths, slots.transpose(1, 2, 0)[0], counts.transpose(1, 0), tiles)

    def along(a, k):
        ways = [(z, (z + k) % Z) for z in range(Z)] + [(Z + z, Z + (z - k) % Z) for z in range(Z)]
        return lax.ppermute(a, ("core", "z"), ways)

    def across(a, k):
        return lax.ppermute(a, "x", turn(X, k))

    def swap(a):
        return lax.ppermute(a, "core", turn(CORES, 1))

    near = {0: own} | {k: along(own, k) for k in (1, -1, 2, -2)}
    far = {0: swap(own)}
    flat, _ = tied(tokens.reshape(queries * query_len, width), own)
    embeds, embeds_here = encode(flat, w_in, b_in, w_out, b_out, gain, shift, proj, queries, query_len)
    near[1], near[-1], near[2], near[-2], far[0], embeds = tied(near[1], near[-1], near[2], near[-2], far[0], embeds)
    near[3], near[-3], near[4] = along(near[2], 1), along(near[-2], -1), along(near[2], 2)
    blocks = {0: embeds_here} | {i: across(embeds, k) for i, k in ((1, 1), (2, -1), (3, 2))}
    far |= {k: swap(near[k]) for k in (1, -1, 2, -2)}
    args = (half, length, queries)

    def mine(*ks):
        return [(near[k], near[k], k, False) for k in ks]

    def others(*ks):
        return [(far[k], near[k if k == 4 else -k], -k, True) for k in ks]

    found = score({0: blocks[0]}, mine(0, 1, -1, 2, -2) + others(0), *args)
    found, blocks[1], blocks[2], blocks[3] = tied(found, blocks[1], blocks[2], blocks[3])
    three = {i: blocks[i] for i in (1, 2, 3)}
    found = score(three, mine(0, 1, -1, 2, -2) + others(0), *args, begun=found)
    found, near[3], near[-3], near[4] = tied(found, near[3], near[-3], near[4])
    far |= {k: swap(near[k]) for k in (3, -3, 4)}
    found = score(blocks, others(1, -1, 2, -2), *args, begun=found)
    found = score(blocks, mine(3, -3, 4) + others(3, -3, 4), *args, begun=found)
    sources = [found] + [across(found, k) for k in (1, -1, 2)]
    return finish(sources, queries).transpose(0, 2, 1)


def solution(mesh):
    fine = Mesh(mesh.devices.reshape(Y, CORES, X, Z), ("y", "core", "x", "z"))
    group, shard = ("y", "core"), ("x", "z")
    placed = (P(group + shard),) + (P(),) * 7 + (P(shard), P(shard), P(group, shard), P(group, shard))
    return jax.shard_map(shards, mesh=fine, in_specs=placed, out_specs=P(group + shard), check_vma=False)
```

```python
import functools

import jax
import jax.numpy as jnp
from jax import lax
from jax.experimental import pallas as pl
from jax.experimental.pallas import tpu as pltpu
from jax.sharding import Mesh
from jax.sharding import PartitionSpec as P

Y, CORES, X, Z = 4, 2, 4, 8
HALF_ROOT = 0.7071067811865476


def turn(size, step):
    return [(i, (i + step) % size) for i in range(size)]


def gelu(pre):
    return 0.5 * pre * (1.0 + lax.erf(pre * jnp.float32(HALF_ROOT)))


VM = pl.BlockSpec(memory_space=pltpu.VMEM)
FREE = pl.CostEstimate(flops=1000, bytes_accessed=1000, transcendentals=0)


def ffn_kernel(tok, w_in, b_in, w_out, b_out, gain, shift, proj, out, again, acc, turned, *, queries, tokens):
    step = pl.program_id(0)
    chunk = w_in.shape[1]
    start = pl.multiple_of(step * chunk, chunk)
    pre = jnp.dot(tok[...], w_in[...], preferred_element_type=jnp.float32) + b_in[pl.ds(start, chunk)][None, :]
    hidden = gelu(pre).astype(jnp.bfloat16)
    part = jnp.dot(hidden, w_out[...], preferred_element_type=jnp.float32)

    @pl.when(step == 0)
    def _():
        acc[...] = part

    @pl.when(step > 0)
    def _():
        acc[...] += part

    @pl.when(step == pl.num_programs(0) - 1)
    def _():
        total = acc[...] + b_out[...][None, :] + tok[...].astype(jnp.float32)
        diff = total - jnp.mean(total, axis=-1, keepdims=True)
        spread = jnp.mean(diff * diff, axis=-1, keepdims=True)
        normed = (diff * lax.rsqrt(spread + 1e-5) * gain[...][None, :] + shift[...][None, :]).astype(jnp.bfloat16)
        projected = jnp.dot(normed, proj[...], preferred_element_type=jnp.float32)
        scale = lax.rsqrt(jnp.sum(projected * projected, axis=-1, keepdims=True) + 1e-6)
        embeds = projected * scale
        for q in range(queries):
            turned[pl.ds(q, tokens, stride=queries), :] = embeds[q * tokens : (q + 1) * tokens, :]
        out[...] = turned[...].astype(jnp.bfloat16)
        again[...] = turned[...].astype(jnp.bfloat16)


def encode(tok, w_in, b_in, w_out, b_out, gain, shift, proj, queries, tokens, chunk=1024):
    rows, width = tok.shape

    def whole(a):
        return pl.BlockSpec(a.shape, lambda j: (0,) * a.ndim)

    return pl.pallas_call(
        functools.partial(ffn_kernel, queries=queries, tokens=tokens),
        grid=(w_in.shape[1] // chunk,),
        in_specs=[
            whole(tok),
            pl.BlockSpec((width, chunk), lambda j: (0, j)),
            whole(b_in),
            pl.BlockSpec((chunk, width), lambda j: (j, 0)),
            whole(b_out),
            whole(gain),
            whole(shift),
            whole(proj),
        ],
        out_specs=[pl.BlockSpec((rows, proj.shape[1]), lambda j: (0, 0)), VM],
        out_shape=[jax.ShapeDtypeStruct((rows, proj.shape[1]), jnp.bfloat16)] * 2,
        scratch_shapes=[pltpu.VMEM((rows, width), jnp.float32), pltpu.VMEM((rows, proj.shape[1]), jnp.float32)],
        compiler_params=pltpu.CompilerParams(vmem_limit_bytes=60 << 20),
        cost_estimate=FREE,
        name="encode",
    )(tok, w_in, b_in, w_out, b_out, gain, shift, proj)


def parcel_kernel(sizes, slots, counts, tiles, out, *, half):
    count, length = tiles.shape[:2]
    core = lax.axis_index("core")
    column = lax.broadcasted_iota(jnp.int32, tiles.shape[1:], 0)
    for t in range(half):
        tile = tiles[core * half + t].astype(jnp.float32)
        size = sizes[core * half + t]
        out[t * length : (t + 1) * length, :] = jnp.where(column < size, tile, tile[0:1, :]).astype(jnp.bfloat16)
    order = lax.broadcasted_iota(jnp.int32, slots.shape, 0)
    codes = jnp.where(order < counts[...], slots[...], count).astype(jnp.float32)
    lines = []
    for x in range(X):
        lines += [codes[:, x * 128 : (x + 1) * 128], jnp.zeros((4, 128), jnp.float32)]
    out[half * length : half * length + 8 * X, :] = jnp.concatenate(lines, axis=0).astype(jnp.bfloat16)


def make_parcel(sizes, slots, counts, tiles):
    count, length, dims = tiles.shape
    half = count // CORES
    return pl.pallas_call(
        functools.partial(parcel_kernel, half=half),
        in_specs=[pl.BlockSpec(memory_space=pltpu.SMEM), VM, VM, VM],
        out_specs=VM,
        out_shape=jax.ShapeDtypeStruct((half * length + 8 * X, dims), jnp.bfloat16),
        name="parcel",
    )(sizes, slots, counts, tiles)


SENDER = (0, X - 1, 1, 2)


def score_kernel(*refs, senders, items, arrays, tiles, length, group, chained):
    s, n = len(senders), len(items)
    blocks, held, out, acc = refs[:s], refs[s : s + arrays], refs[-2], refs[-1]
    rows = tiles * length
    lane_group = lax.broadcasted_iota(jnp.int32, (8, 128), 1) // group
    row = lax.broadcasted_iota(jnp.int32, (8, 128), 0)
    core, x, z = lax.axis_index("core"), lax.axis_index("x"), lax.axis_index("z")
    acc[...] = jnp.zeros_like(acc)

    for sender, queries in zip(senders, blocks):
        block = queries[...]
        here = lane_group == lax.rem(x + SENDER[sender], X)
        for n, (parcel, *_) in enumerate(items):
            similar = lax.dot_general(
                held[parcel][0:rows, :], block, (((1,), (1,)), ((), ())), preferred_element_type=jnp.float32
            )
            sums = []
            for t in range(tiles):
                best = jnp.max(similar[t * length : (t + 1) * length], axis=0, keepdims=True)
                sums.append(best[:, 0:128] + best[:, 128:256] + best[:, 256:384] + best[:, 384:512])
            sums = jnp.concatenate(sums + [jnp.zeros((8 - tiles, 128), jnp.float32)], axis=0)
            sums = sums + pltpu.roll(sums, 64, 1)
            sums = sums + pltpu.roll(sums, 32, 1)
            sums = sums + pltpu.roll(sums, 16, 1)
            acc[n] = jnp.where(here, sums, acc[n])

    out[...] = refs[s + arrays][...] if chained else jnp.zeros_like(out)
    way = 2 * core - 1
    for n, (_, label, steps, far) in enumerate(items):
        codes = held[label][rows : rows + 8 * X, :].astype(jnp.float32)
        code = jnp.full((8, 128), -1.0, jnp.float32)
        for d in range(X):
            turned = pltpu.roll(codes[d * 8 : d * 8 + 8], lax.rem((d - z) * group + 128, 128), 1)
            code = jnp.where(lane_group == d, turned, code)
        code = code.astype(jnp.int32) - tiles * (1 - core if far else core)
        shard = lax.rem(z + steps * way + Z, Z)
        for c in range(4):
            picked = (code[c : c + 1] == row) & (row < tiles)
            line = jnp.sum(jnp.where(picked, acc[n], 0.0), axis=0, keepdims=True)
            out[pl.ds(c * Z + shard, 1), :] += line


def score(blocks, items, tiles, length, group, begun=None):
    held = []

    def at(array):
        for i, one in enumerate(held):
            if one is array:
                return i
        held.append(array)
        return len(held) - 1

    plan = tuple((at(parcel), at(label), steps, far) for parcel, label, steps, far in items)
    more = [] if begun is None else [begun]
    return pl.pallas_call(
        functools.partial(
            score_kernel,
            senders=tuple(blocks),
            items=plan,
            arrays=len(held),
            tiles=tiles,
            length=length,
            group=group,
            chained=begun is not None,
        ),
        in_specs=[VM] * (len(blocks) + len(held) + len(more)),
        out_specs=VM,
        out_shape=jax.ShapeDtypeStruct((4 * Z, 128), jnp.float32),
        scratch_shapes=[pltpu.VMEM((len(plan), 8, 128), jnp.float32)],
        compiler_params=pltpu.CompilerParams(vmem_limit_bytes=32 << 20),
        cost_estimate=FREE,
        name=f"score_{len(blocks)}_{len(plan)}",
    )(*blocks.values(), *held, *more)


def finish_kernel(*refs, group):
    sources, out, table = refs[:4], refs[4], refs[5]
    x = lax.axis_index("x")
    for sender, source in zip(SENDER, sources):
        lines = pltpu.roll(source[...], lax.rem(128 - x * group, 128), 1)
        shard = lax.rem(x + sender, X) * Z
        for c in range(4):
            table[pl.ds(pl.multiple_of(c * X * Z + shard, Z), Z), :] = lines[c * Z : (c + 1) * Z]
    turned = table[...].T
    for c in range(4):
        out[:, c, :] = turned[0:group, c * X * Z : (c + 1) * X * Z]


def finish(sources, group):
    return pl.pallas_call(
        functools.partial(finish_kernel, group=group),
        in_specs=[VM] * 4,
        out_specs=VM,
        out_shape=jax.ShapeDtypeStruct((group, 4, X * Z), jnp.float32),
        scratch_shapes=[pltpu.VMEM((128, 128), jnp.float32)],
        compiler_params=pltpu.CompilerParams(vmem_limit_bytes=8 << 20),
        name="finish",
    )(*sources)


def tied(*arrays):
    return lax.optimization_barrier(arrays)


def shards(tokens, w_in, b_in, w_out, b_out, gain, shift, proj, tiles, lengths, slots, counts):
    queries, query_len, width = tokens.shape
    count, length, dims = tiles.shape
    half = count // CORES
    own = make_parcel(lengths, slots.transpose(1, 2, 0)[0], counts.transpose(1, 0), tiles)

    def along(a, k):
        ways = [(z, (z + k) % Z) for z in range(Z)] + [(Z + z, Z + (z - k) % Z) for z in range(Z)]
        return lax.ppermute(a, ("core", "z"), ways)

    def across(a, k):
        return lax.ppermute(a, "x", turn(X, k))

    def swap(a):
        return lax.ppermute(a, "core", turn(CORES, 1))

    near = {0: own} | {k: along(own, k) for k in (1, -1, 2, -2)}
    far = {0: swap(own)}
    flat, _ = tied(tokens.reshape(queries * query_len, width), own)
    embeds, embeds_here = encode(flat, w_in, b_in, w_out, b_out, gain, shift, proj, queries, query_len)
    near[1], near[-1], near[2], near[-2], far[0], embeds = tied(near[1], near[-1], near[2], near[-2], far[0], embeds)
    blocks = {0: embeds_here} | {i: across(embeds, k) for i, k in ((1, 1), (2, -1), (3, 2))}
    far |= {k: swap(near[k]) for k in (1, -1, 2, -2)}
    args = (half, length, queries)

    def mine(*ks):
        return [(near[k], near[k], k, False) for k in ks]

    def others(*ks):
        return [(far[k], near[k if k == 4 else -k], -k, True) for k in ks]

    found = score({0: blocks[0]}, mine(0, 1, -1, 2, -2) + others(0), *args)
    found, blocks[1], blocks[2], blocks[3], near[2] = tied(found, blocks[1], blocks[2], blocks[3], near[2])
    near[3] = along(near[2], 1)
    three = {i: blocks[i] for i in (1, 2, 3)}
    found = score(three, mine(0, 1, -1), *args, begun=found)
    found, near[-2] = tied(found, near[-2])
    near[-3] = along(near[-2], -1)
    found = score(three, mine(2, -2) + others(0), *args, begun=found)
    found, near[2], near[3] = tied(found, near[2], near[3])
    near[4] = along(near[2], 2)
    far[3] = swap(near[3])
    found = score(blocks, others(1, -1, 2, -2), *args, begun=found)
    found, near[-3] = tied(found, near[-3])
    far[-3] = swap(near[-3])
    found = score(blocks, mine(3, -3), *args, begun=found)
    found, near[4] = tied(found, near[4])
    far[4] = swap(near[4])
    found = score(blocks, mine(4) + others(3, -3), *args, begun=found)
    found = score(blocks, others(4), *args, begun=found)
    sources = [found] + [across(found, k) for k in (1, -1, 2)]
    return finish(sources, queries).transpose(0, 2, 1)


def solution(mesh):
    fine = Mesh(mesh.devices.reshape(Y, CORES, X, Z), ("y", "core", "x", "z"))
    group, shard = ("y", "core"), ("x", "z")
    placed = (P(group + shard),) + (P(),) * 7 + (P(shard), P(shard), P(group, shard), P(group, shard))
    return jax.shard_map(shards, mesh=fine, in_specs=placed, out_specs=P(group + shard), check_vma=False)
```

```python
import functools

import jax
import jax.numpy as jnp
from jax import lax
from jax.experimental import pallas as pl
from jax.experimental.pallas import tpu as pltpu
from jax.sharding import Mesh
from jax.sharding import PartitionSpec as P

Y, CORES, X, Z = 4, 2, 4, 8
HALF_ROOT = 0.7071067811865476


def turn(size, step):
    return [(i, (i + step) % size) for i in range(size)]


def gelu(pre):
    return 0.5 * pre * (1.0 + lax.erf(pre * jnp.float32(HALF_ROOT)))


FREE = pl.CostEstimate(flops=1000, bytes_accessed=1000, transcendentals=0)


def ffn_kernel(tok, w_in, b_in, w_out, b_out, gain, shift, proj, out, acc, turned, *, queries, tokens):
    step = pl.program_id(0)
    chunk = w_in.shape[1]
    start = pl.multiple_of(step * chunk, chunk)
    pre = jnp.dot(tok[...], w_in[...], preferred_element_type=jnp.float32) + b_in[pl.ds(start, chunk)][None, :]
    hidden = gelu(pre).astype(jnp.bfloat16)
    part = jnp.dot(hidden, w_out[...], preferred_element_type=jnp.float32)

    @pl.when(step == 0)
    def _():
        acc[...] = part

    @pl.when(step > 0)
    def _():
        acc[...] += part

    @pl.when(step == pl.num_programs(0) - 1)
    def _():
        total = acc[...] + b_out[...][None, :] + tok[...].astype(jnp.float32)
        diff = total - jnp.mean(total, axis=-1, keepdims=True)
        spread = jnp.mean(diff * diff, axis=-1, keepdims=True)
        normed = (diff * lax.rsqrt(spread + 1e-5) * gain[...][None, :] + shift[...][None, :]).astype(jnp.bfloat16)
        projected = jnp.dot(normed, proj[...], preferred_element_type=jnp.float32)
        scale = lax.rsqrt(jnp.sum(projected * projected, axis=-1, keepdims=True) + 1e-6)
        embeds = projected * scale
        for q in range(queries):
            turned[pl.ds(q, tokens, stride=queries), :] = embeds[q * tokens : (q + 1) * tokens, :]
        out[...] = turned[...].astype(jnp.bfloat16)


def encode(tok, w_in, b_in, w_out, b_out, gain, shift, proj, queries, tokens, chunk=1024):
    rows, width = tok.shape

    def whole(a):
        return pl.BlockSpec(a.shape, lambda j: (0,) * a.ndim)

    return pl.pallas_call(
        functools.partial(ffn_kernel, queries=queries, tokens=tokens),
        grid=(w_in.shape[1] // chunk,),
        in_specs=[
            whole(tok),
            pl.BlockSpec((width, chunk), lambda j: (0, j)),
            whole(b_in),
            pl.BlockSpec((chunk, width), lambda j: (j, 0)),
            whole(b_out),
            whole(gain),
            whole(shift),
            whole(proj),
        ],
        out_specs=pl.BlockSpec((rows, proj.shape[1]), lambda j: (0, 0)),
        out_shape=jax.ShapeDtypeStruct((rows, proj.shape[1]), jnp.bfloat16),
        scratch_shapes=[pltpu.VMEM((rows, width), jnp.float32), pltpu.VMEM((rows, proj.shape[1]), jnp.float32)],
        compiler_params=pltpu.CompilerParams(vmem_limit_bytes=60 << 20),
        cost_estimate=FREE,
        name="encode",
    )(tok, w_in, b_in, w_out, b_out, gain, shift, proj)


def parcel_kernel(sizes, slots, counts, tiles, out, *, half):
    count, length = tiles.shape[:2]
    core = lax.axis_index("core")
    column = lax.broadcasted_iota(jnp.int32, tiles.shape[1:], 0)
    for t in range(half):
        tile = tiles[core * half + t].astype(jnp.float32)
        size = sizes[core * half + t]
        out[t * length : (t + 1) * length, :] = jnp.where(column < size, tile, tile[0:1, :]).astype(jnp.bfloat16)
    order = lax.broadcasted_iota(jnp.int32, slots.shape, 0)
    codes = jnp.where(order < counts[...], slots[...], count).astype(jnp.float32)
    lines = []
    for x in range(X):
        lines += [codes[:, x * 128 : (x + 1) * 128], jnp.zeros((4, 128), jnp.float32)]
    out[half * length : half * length + 8 * X, :] = jnp.concatenate(lines, axis=0).astype(jnp.bfloat16)


VM = pl.BlockSpec(memory_space=pltpu.VMEM)


def make_parcel(sizes, slots, counts, tiles):
    count, length, dims = tiles.shape
    half = count // CORES
    return pl.pallas_call(
        functools.partial(parcel_kernel, half=half),
        in_specs=[pl.BlockSpec(memory_space=pltpu.SMEM), VM, VM, VM],
        out_specs=VM,
        out_shape=jax.ShapeDtypeStruct((half * length + 8 * X, dims), jnp.bfloat16),
        name="parcel",
    )(sizes, slots, counts, tiles)


SENDER = (0, X - 1, 1, 2)


def score_kernel(*refs, senders, items, arrays, tiles, length, group, chained):
    s, n = len(senders), len(items)
    blocks, held, out, acc, fetched, arrived = refs[:s], refs[s : s + arrays], *refs[-4:]
    fetch = pltpu.make_async_copy(blocks[-1], fetched, arrived)
    fetch.start()
    rows = tiles * length
    lane_group = lax.broadcasted_iota(jnp.int32, (8, 128), 1) // group
    row = lax.broadcasted_iota(jnp.int32, (8, 128), 0)
    core, x, z = lax.axis_index("core"), lax.axis_index("x"), lax.axis_index("z")
    acc[...] = jnp.zeros_like(acc)

    for sender, queries in zip(senders, blocks):
        if queries is blocks[-1]:
            fetch.wait()
            queries = fetched
        block = queries[...]
        here = lane_group == lax.rem(x + SENDER[sender], X)
        for n, (parcel, *_) in enumerate(items):
            similar = lax.dot_general(
                held[parcel][0:rows, :], block, (((1,), (1,)), ((), ())), preferred_element_type=jnp.float32
            )
            sums = []
            for t in range(tiles):
                best = jnp.max(similar[t * length : (t + 1) * length], axis=0, keepdims=True)
                sums.append(best[:, 0:128] + best[:, 128:256] + best[:, 256:384] + best[:, 384:512])
            sums = jnp.concatenate(sums + [jnp.zeros((8 - tiles, 128), jnp.float32)], axis=0)
            sums = sums + pltpu.roll(sums, 64, 1)
            sums = sums + pltpu.roll(sums, 32, 1)
            sums = sums + pltpu.roll(sums, 16, 1)
            acc[n] = jnp.where(here, sums, acc[n])

    out[...] = refs[s + arrays][...] if chained else jnp.zeros_like(out)
    way = 2 * core - 1
    for n, (_, label, steps, far) in enumerate(items):
        codes = held[label][rows : rows + 8 * X, :].astype(jnp.float32)
        code = jnp.full((8, 128), -1.0, jnp.float32)
        for d in range(X):
            turned = pltpu.roll(codes[d * 8 : d * 8 + 8], lax.rem((d - z) * group + 128, 128), 1)
            code = jnp.where(lane_group == d, turned, code)
        code = code.astype(jnp.int32) - tiles * (1 - core if far else core)
        shard = lax.rem(z + steps * way + Z, Z)
        for c in range(4):
            picked = (code[c : c + 1] == row) & (row < tiles)
            line = jnp.sum(jnp.where(picked, acc[n], 0.0), axis=0, keepdims=True)
            out[pl.ds(c * Z + shard, 1), :] += line


def score(blocks, items, tiles, length, group, begun=None):
    held = []

    def at(array):
        for i, one in enumerate(held):
            if one is array:
                return i
        held.append(array)
        return len(held) - 1

    plan = tuple((at(parcel), at(label), steps, far) for parcel, label, steps, far in items)
    more = [] if begun is None else [begun]
    return pl.pallas_call(
        functools.partial(
            score_kernel,
            senders=tuple(blocks),
            items=plan,
            arrays=len(held),
            tiles=tiles,
            length=length,
            group=group,
            chained=begun is not None,
        ),
        in_specs=[VM] * (len(blocks) - 1) + [pl.BlockSpec(memory_space=pltpu.HBM)] + [VM] * (len(held) + len(more)),
        out_specs=VM,
        out_shape=jax.ShapeDtypeStruct((4 * Z, 128), jnp.float32),
        scratch_shapes=[
            pltpu.VMEM((len(plan), 8, 128), jnp.float32),
            pltpu.VMEM((512, 128), jnp.bfloat16),
            pltpu.SemaphoreType.DMA,
        ],
        compiler_params=pltpu.CompilerParams(vmem_limit_bytes=32 << 20),
        cost_estimate=FREE,
        name=f"score_{len(blocks)}_{len(plan)}",
    )(*blocks.values(), *held, *more)


def finish_kernel(*refs, group):
    sources, out, table = refs[:4], refs[4], refs[5]
    x = lax.axis_index("x")
    for sender, source in zip(SENDER, sources):
        lines = pltpu.roll(source[...], lax.rem(128 - x * group, 128), 1)
        shard = lax.rem(x + sender, X) * Z
        for c in range(4):
            table[pl.ds(pl.multiple_of(c * X * Z + shard, Z), Z), :] = lines[c * Z : (c + 1) * Z]
    turned = table[...].T
    for c in range(4):
        out[:, c, :] = turned[0:group, c * X * Z : (c + 1) * X * Z]


def finish(sources, group):
    return pl.pallas_call(
        functools.partial(finish_kernel, group=group),
        in_specs=[VM] * 4,
        out_specs=VM,
        out_shape=jax.ShapeDtypeStruct((group, 4, X * Z), jnp.float32),
        scratch_shapes=[pltpu.VMEM((128, 128), jnp.float32)],
        compiler_params=pltpu.CompilerParams(vmem_limit_bytes=8 << 20),
        name="finish",
    )(*sources)


def tied(*arrays):
    return lax.optimization_barrier(arrays)


def shards(tokens, w_in, b_in, w_out, b_out, gain, shift, proj, tiles, lengths, slots, counts):
    queries, query_len, width = tokens.shape
    count, length, dims = tiles.shape
    half = count // CORES
    own = make_parcel(lengths, slots.transpose(1, 2, 0)[0], counts.transpose(1, 0), tiles)

    def along(a, k):
        ways = [(z, (z + k) % Z) for z in range(Z)] + [(Z + z, Z + (z - k) % Z) for z in range(Z)]
        return lax.ppermute(a, ("core", "z"), ways)

    def across(a, k):
        return lax.ppermute(a, "x", turn(X, k))

    def swap(a):
        return lax.ppermute(a, "core", turn(CORES, 1))

    near = {0: own} | {k: along(own, k) for k in (1, -1, 2, -2)}
    far = {0: swap(own)}
    flat, _ = tied(tokens.reshape(queries * query_len, width), own)
    embeds = encode(flat, w_in, b_in, w_out, b_out, gain, shift, proj, queries, query_len)
    near[1], near[-1], near[2], near[-2], far[0], embeds = tied(near[1], near[-1], near[2], near[-2], far[0], embeds)
    near[3], near[-3], near[4] = along(near[2], 1), along(near[-2], -1), along(near[2], 2)
    blocks = {i: across(embeds, k) for i, k in ((1, 1), (2, -1), (3, 2))} | {0: embeds}
    far |= {k: swap(near[k]) for k in (1, -1, 2, -2)}
    args = (half, length, queries)

    def mine(*ks):
        return [(near[k], near[k], k, False) for k in ks]

    def others(*ks):
        return [(far[k], near[k if k == 4 else -k], -k, True) for k in ks]

    found = score(blocks, mine(0, 1, -1, 2, -2) + others(0), *args)
    found, near[3], near[-3], near[4] = tied(found, near[3], near[-3], near[4])
    far |= {k: swap(near[k]) for k in (3, -3, 4)}
    found = score(blocks, others(1, -1, 2, -2), *args, begun=found)
    found = score(blocks, mine(3, -3, 4) + others(3, -3, 4), *args, begun=found)
    sources = [found] + [across(found, k) for k in (1, -1, 2)]
    return finish(sources, queries).transpose(0, 2, 1)


def solution(mesh):
    fine = Mesh(mesh.devices.reshape(Y, CORES, X, Z), ("y", "core", "x", "z"))
    group, shard = ("y", "core"), ("x", "z")
    placed = (P(group + shard),) + (P(),) * 7 + (P(shard), P(shard), P(group, shard), P(group, shard))
    return jax.shard_map(shards, mesh=fine, in_specs=placed, out_specs=P(group + shard), check_vma=False)
```

```python
import functools

import jax
import jax.numpy as jnp
from jax import lax
from jax.experimental import pallas as pl
from jax.experimental.pallas import tpu as pltpu
from jax.sharding import Mesh
from jax.sharding import PartitionSpec as P

Y, CORES, X, Z = 4, 2, 4, 8
HALF_ROOT = 0.7071067811865476


def turn(size, step):
    return [(i, (i + step) % size) for i in range(size)]


def gelu(pre):
    return 0.5 * pre * (1.0 + lax.erf(pre * jnp.float32(HALF_ROOT)))


FREE = pl.CostEstimate(flops=1000, bytes_accessed=1000, transcendentals=0)


def ffn_kernel(tok, w_in, b_in, w_out, b_out, gain, shift, proj, out, acc, turned, *, queries, tokens):
    step = pl.program_id(0)
    chunk = w_in.shape[1]
    start = pl.multiple_of(step * chunk, chunk)
    pre = jnp.dot(tok[...], w_in[...], preferred_element_type=jnp.float32) + b_in[pl.ds(start, chunk)][None, :]
    hidden = gelu(pre).astype(jnp.bfloat16)
    part = jnp.dot(hidden, w_out[...], preferred_element_type=jnp.float32)

    @pl.when(step == 0)
    def _():
        acc[...] = part

    @pl.when(step > 0)
    def _():
        acc[...] += part

    @pl.when(step == pl.num_programs(0) - 1)
    def _():
        total = acc[...] + b_out[...][None, :] + tok[...].astype(jnp.float32)
        diff = total - jnp.mean(total, axis=-1, keepdims=True)
        spread = jnp.mean(diff * diff, axis=-1, keepdims=True)
        normed = (diff * lax.rsqrt(spread + 1e-5) * gain[...][None, :] + shift[...][None, :]).astype(jnp.bfloat16)
        projected = jnp.dot(normed, proj[...], preferred_element_type=jnp.float32)
        scale = lax.rsqrt(jnp.sum(projected * projected, axis=-1, keepdims=True) + 1e-6)
        embeds = projected * scale
        for q in range(queries):
            turned[pl.ds(q, tokens, stride=queries), :] = embeds[q * tokens : (q + 1) * tokens, :]
        out[...] = turned[...].astype(jnp.bfloat16)


def encode(tok, w_in, b_in, w_out, b_out, gain, shift, proj, queries, tokens, chunk=1536):
    rows, width = tok.shape

    def whole(a):
        return pl.BlockSpec(a.shape, lambda j: (0,) * a.ndim)

    return pl.pallas_call(
        functools.partial(ffn_kernel, queries=queries, tokens=tokens),
        grid=(w_in.shape[1] // chunk,),
        in_specs=[
            whole(tok),
            pl.BlockSpec((width, chunk), lambda j: (0, j)),
            whole(b_in),
            pl.BlockSpec((chunk, width), lambda j: (j, 0)),
            whole(b_out),
            whole(gain),
            whole(shift),
            whole(proj),
        ],
        out_specs=pl.BlockSpec((rows, proj.shape[1]), lambda j: (0, 0)),
        out_shape=jax.ShapeDtypeStruct((rows, proj.shape[1]), jnp.bfloat16),
        scratch_shapes=[pltpu.VMEM((rows, width), jnp.float32), pltpu.VMEM((rows, proj.shape[1]), jnp.float32)],
        compiler_params=pltpu.CompilerParams(vmem_limit_bytes=60 << 20),
        cost_estimate=FREE,
        name="encode",
    )(tok, w_in, b_in, w_out, b_out, gain, shift, proj)


def parcel_kernel(sizes, slots, counts, tiles, out, other, *, half):
    count, length = tiles.shape[:2]
    core = lax.axis_index("core")
    column = lax.broadcasted_iota(jnp.int32, tiles.shape[1:], 0)
    for side, to in ((core, out), (1 - core, other)):
        for t in range(half):
            tile = tiles[side * half + t].astype(jnp.float32)
            size = sizes[side * half + t]
            to[t * length : (t + 1) * length, :] = jnp.where(column < size, tile, tile[0:1, :]).astype(jnp.bfloat16)
    order = lax.broadcasted_iota(jnp.int32, slots.shape, 0)
    codes = jnp.where(order < counts[...], slots[...], count).astype(jnp.float32)
    lines = []
    for x in range(X):
        lines += [codes[:, x * 128 : (x + 1) * 128], jnp.zeros((4, 128), jnp.float32)]
    out[half * length : half * length + 8 * X, :] = jnp.concatenate(lines, axis=0).astype(jnp.bfloat16)


VM = pl.BlockSpec(memory_space=pltpu.VMEM)


def make_parcel(sizes, slots, counts, tiles):
    count, length, dims = tiles.shape
    half = count // CORES
    return pl.pallas_call(
        functools.partial(parcel_kernel, half=half),
        in_specs=[pl.BlockSpec(memory_space=pltpu.SMEM), VM, VM, VM],
        out_specs=[VM, VM],
        out_shape=[jax.ShapeDtypeStruct((half * length + r, dims), jnp.bfloat16) for r in (8 * X, 0)],
        name="parcel",
    )(sizes, slots, counts, tiles)


SENDER = (0, X - 1, 1, 2)


def score_kernel(*refs, senders, items, arrays, tiles, length, group, chained, keep):
    s, n = len(senders), len(items)
    blocks, held, out = refs[:s], refs[s : s + arrays], refs[-2 if keep else -1]
    if keep:
        refs[-1][...] = blocks[-1][...]
    rows = tiles * length
    lane_group = lax.broadcasted_iota(jnp.int32, (8, 128), 1) // group
    row = lax.broadcasted_iota(jnp.int32, (8, 128), 0)
    core, x, z = lax.axis_index("core"), lax.axis_index("x"), lax.axis_index("z")
    best_of = [jnp.zeros((8, 128), jnp.float32)] * n
    for sender, queries in zip(senders, blocks):
        block = queries[...]
        here = lane_group == lax.rem(x + SENDER[sender], X)
        for i, (parcel, *_) in enumerate(items):
            similar = lax.dot_general(
                held[parcel][0:rows, :], block, (((1,), (1,)), ((), ())), preferred_element_type=jnp.float32
            )
            sums = []
            for t in range(tiles):
                best = jnp.max(similar[t * length : (t + 1) * length], axis=0, keepdims=True)
                sums.append(best[:, 0:128] + best[:, 128:256] + best[:, 256:384] + best[:, 384:512])
            sums = jnp.concatenate(sums + [jnp.zeros((8 - tiles, 128), jnp.float32)], axis=0)
            sums = sums + pltpu.roll(sums, 64, 1)
            sums = sums + pltpu.roll(sums, 32, 1)
            sums = sums + pltpu.roll(sums, 16, 1)
            best_of[i] = jnp.where(here, sums, best_of[i])

    found = [refs[s + arrays][c * Z : (c + 1) * Z] if chained else jnp.zeros((Z, 128), jnp.float32) for c in range(4)]
    way = 2 * core - 1
    for i, (_, label, steps, far) in enumerate(items):
        codes = held[label][rows : rows + 8 * X, :].astype(jnp.float32)
        code = jnp.full((8, 128), -1.0, jnp.float32)
        for d in range(X):
            turned = pltpu.roll(codes[d * 8 : d * 8 + 8], lax.rem((d - z) * group + 128, 128), 1)
            code = jnp.where(lane_group == d, turned, code)
        code = code.astype(jnp.int32) - tiles * (1 - core if far else core)
        shard = lax.rem(z + steps * way + Z, Z)
        for c in range(4):
            picked = (code[c : c + 1] == row) & (row < tiles)
            line = jnp.sum(jnp.where(picked, best_of[i], 0.0), axis=0, keepdims=True)
            found[c] = found[c] + jnp.where(row == shard, line, 0.0)
    for c in range(4):
        out[c * Z : (c + 1) * Z] = found[c]


def score(blocks, items, tiles, length, group, begun=None, keep=False):
    held = []

    def at(array):
        for i, one in enumerate(held):
            if one is array:
                return i
        held.append(array)
        return len(held) - 1

    plan = tuple((at(parcel), at(label), steps, far) for parcel, label, steps, far in items)
    more = [] if begun is None else [begun]
    shape = jax.ShapeDtypeStruct((4 * Z, 128), jnp.float32)
    return pl.pallas_call(
        functools.partial(
            score_kernel,
            senders=tuple(blocks),
            items=plan,
            arrays=len(held),
            tiles=tiles,
            length=length,
            group=group,
            chained=begun is not None,
            keep=keep,
        ),
        in_specs=[VM] * (len(blocks) + len(held) + len(more)),
        out_specs=[VM, VM] if keep else VM,
        out_shape=[shape, jax.ShapeDtypeStruct((512, 128), jnp.bfloat16)] if keep else shape,
        compiler_params=pltpu.CompilerParams(vmem_limit_bytes=32 << 20),
        cost_estimate=FREE,
        name=f"score_{len(blocks)}_{len(plan)}",
    )(*blocks.values(), *held, *more)


def finish_kernel(*refs, group):
    sources, out, table = refs[:4], refs[4], refs[5]
    x = lax.axis_index("x")
    for sender, source in zip(SENDER, sources):
        lines = pltpu.roll(source[...], lax.rem(128 - x * group, 128), 1)
        shard = lax.rem(x + sender, X) * Z
        for c in range(4):
            table[pl.ds(pl.multiple_of(c * X * Z + shard, Z), Z), :] = lines[c * Z : (c + 1) * Z]
    turned = table[...].T
    for c in range(4):
        out[:, c, :] = turned[0:group, c * X * Z : (c + 1) * X * Z]


def finish(sources, group):
    return pl.pallas_call(
        functools.partial(finish_kernel, group=group),
        in_specs=[VM] * 4,
        out_specs=VM,
        out_shape=jax.ShapeDtypeStruct((group, 4, X * Z), jnp.float32),
        scratch_shapes=[pltpu.VMEM((128, 128), jnp.float32)],
        compiler_params=pltpu.CompilerParams(vmem_limit_bytes=8 << 20),
        name="finish",
    )(*sources)


def tied(*arrays):
    return lax.optimization_barrier(arrays)


def shards(tokens, w_in, b_in, w_out, b_out, gain, shift, proj, tiles, lengths, slots, counts):
    queries, query_len, width = tokens.shape
    count, length, dims = tiles.shape
    half = count // CORES
    own, own_far = make_parcel(lengths, slots.transpose(1, 2, 0)[0], counts.transpose(1, 0), tiles)

    def along(a, k):
        ways = [(z, (z + k) % Z) for z in range(Z)] + [(Z + z, Z + (z - k) % Z) for z in range(Z)]
        return lax.ppermute(a, ("core", "z"), ways)

    def across(a, k):
        return lax.ppermute(a, "x", turn(X, k))

    def swap(a):
        return lax.ppermute(a, "core", turn(CORES, 1))

    near = {0: own} | {k: along(own, k) for k in (1, -1, 2, -2)}
    far = {0: own_far}
    flat, _ = tied(tokens.reshape(queries * query_len, width), own)
    embeds = encode(flat, w_in, b_in, w_out, b_out, gain, shift, proj, queries, query_len)
    near[1], near[-1], near[2], near[-2], embeds = tied(near[1], near[-1], near[2], near[-2], embeds)
    near[3], near[-3], near[4] = along(near[2], 1), along(near[-2], -1), along(near[2], 2)
    blocks = {i: across(embeds, k) for i, k in ((1, 1), (2, -1), (3, 2))} | {0: embeds}
    args = (half, length, queries)

    def mine(*ks):
        return [(near[k], near[k], k, False) for k in ks]

    def others(*ks):
        return [(far[k], near[k if k == 4 else -k], -k, True) for k in ks]

    early = mine(0, 1, -1, 2, -2) + others(0)
    found, blocks[0] = score({0: blocks[0]}, early, *args, keep=True)
    found, *ready = tied(found, *(near[k] for k in (1, -1, 2, -2)))
    far |= {k: swap(a) for k, a in zip((1, -1, 2, -2), ready)}
    found = score({i: blocks[i] for i in (1, 2, 3)}, early, *args, begun=found)
    found, near[3], near[-3], near[4] = tied(found, near[3], near[-3], near[4])
    far |= {k: swap(near[k]) for k in (3, -3, 4)}
    found = score(blocks, others(1, -1, 2, -2), *args, begun=found)
    found = score(blocks, mine(3, -3, 4) + others(3, -3, 4), *args, begun=found)
    sources = [found] + [across(found, k) for k in (1, -1, 2)]
    return finish(sources, queries).transpose(0, 2, 1)


def solution(mesh):
    fine = Mesh(mesh.devices.reshape(Y, CORES, X, Z), ("y", "core", "x", "z"))
    group, shard = ("y", "core"), ("x", "z")
    placed = (P(group + shard),) + (P(),) * 7 + (P(shard), P(shard), P(group, shard), P(group, shard))
    return jax.shard_map(shards, mesh=fine, in_specs=placed, out_specs=P(group + shard), check_vma=False)
```

```python
import functools

import jax
import jax.numpy as jnp
from jax import lax
from jax.experimental import pallas as pl
from jax.experimental.pallas import tpu as pltpu
from jax.sharding import Mesh
from jax.sharding import PartitionSpec as P

Y, CORES, X, Z = 4, 2, 4, 8
HALF_ROOT = 0.7071067811865476


def turn(size, step):
    return [(i, (i + step) % size) for i in range(size)]


def gelu(pre):
    return 0.5 * pre * (1.0 + lax.erf(pre * jnp.float32(HALF_ROOT)))


FREE = pl.CostEstimate(flops=1000, bytes_accessed=1000, transcendentals=0)


def ffn_kernel(tok, w_in, b_in, w_out, b_out, gain, shift, proj, out, acc, turned, *, queries, tokens):
    step = pl.program_id(0)
    chunk = w_in.shape[1]
    start = pl.multiple_of(step * chunk, chunk)
    pre = jnp.dot(tok[...], w_in[...], preferred_element_type=jnp.float32) + b_in[pl.ds(start, chunk)][None, :]
    hidden = gelu(pre).astype(jnp.bfloat16)
    part = jnp.dot(hidden, w_out[...], preferred_element_type=jnp.float32)

    @pl.when(step == 0)
    def _():
        acc[...] = part

    @pl.when(step > 0)
    def _():
        acc[...] += part

    @pl.when(step == pl.num_programs(0) - 1)
    def _():
        total = acc[...] + b_out[...][None, :] + tok[...].astype(jnp.float32)
        diff = total - jnp.mean(total, axis=-1, keepdims=True)
        spread = jnp.mean(diff * diff, axis=-1, keepdims=True)
        normed = (diff * lax.rsqrt(spread + 1e-5) * gain[...][None, :] + shift[...][None, :]).astype(jnp.bfloat16)
        projected = jnp.dot(normed, proj[...], preferred_element_type=jnp.float32)
        scale = lax.rsqrt(jnp.sum(projected * projected, axis=-1, keepdims=True) + 1e-6)
        embeds = projected * scale
        for q in range(queries):
            turned[pl.ds(q, tokens, stride=queries), :] = embeds[q * tokens : (q + 1) * tokens, :]
        out[...] = turned[...].astype(jnp.bfloat16)


def encode(tok, w_in, b_in, w_out, b_out, gain, shift, proj, queries, tokens, chunk=1536):
    rows, width = tok.shape

    def whole(a):
        return pl.BlockSpec(a.shape, lambda j: (0,) * a.ndim)

    return pl.pallas_call(
        functools.partial(ffn_kernel, queries=queries, tokens=tokens),
        grid=(w_in.shape[1] // chunk,),
        in_specs=[
            whole(tok),
            pl.BlockSpec((width, chunk), lambda j: (0, j)),
            whole(b_in),
            pl.BlockSpec((chunk, width), lambda j: (j, 0)),
            whole(b_out),
            whole(gain),
            whole(shift),
            whole(proj),
        ],
        out_specs=pl.BlockSpec((rows, proj.shape[1]), lambda j: (0, 0)),
        out_shape=jax.ShapeDtypeStruct((rows, proj.shape[1]), jnp.bfloat16),
        scratch_shapes=[pltpu.VMEM((rows, width), jnp.float32), pltpu.VMEM((rows, proj.shape[1]), jnp.float32)],
        compiler_params=pltpu.CompilerParams(vmem_limit_bytes=36 << 20),
        cost_estimate=FREE,
        name="encode",
    )(tok, w_in, b_in, w_out, b_out, gain, shift, proj)


VM = pl.BlockSpec(memory_space=pltpu.VMEM)


def parcel_kernel(facts, tiles, out, other, *, half):
    length = tiles.shape[1]
    core = lax.axis_index("core")
    column = lax.broadcasted_iota(jnp.int32, tiles.shape[1:], 0).astype(jnp.float32)
    lane = lax.broadcasted_iota(jnp.int32, (1, 128), 1)
    for side, to in ((core, out), (1 - core, other)):
        for t in range(half):
            tile = tiles[side * half + t].astype(jnp.float32)
            size = jnp.sum(jnp.where(lane == side * half + t, facts[4:5, 0:128], 0.0), axis=1, keepdims=True)
            to[t * length : (t + 1) * length, :] = jnp.where(column < size, tile, tile[0:1, :]).astype(jnp.bfloat16)
    lines = []
    for x in range(X):
        lines += [facts[0:4, x * 128 : (x + 1) * 128], jnp.zeros((4, 128), jnp.float32)]
    out[half * length : half * length + 8 * X, :] = jnp.concatenate(lines, axis=0).astype(jnp.bfloat16)


def make_parcel(sizes, slots, counts, tiles):
    count, length, dims = tiles.shape
    half = count // CORES
    order = jnp.arange(4, dtype=jnp.int32)[:, None]
    codes = jnp.where(order < counts, slots, count)
    facts = jnp.concatenate([codes, jnp.pad(sizes, (0, codes.shape[1] - count))[None, :]], axis=0).astype(jnp.float32)
    return pl.pallas_call(
        functools.partial(parcel_kernel, half=half),
        in_specs=[VM, VM],
        out_specs=[VM, VM],
        out_shape=[jax.ShapeDtypeStruct((half * length + r, dims), jnp.bfloat16) for r in (8 * X, 0)],
        cost_estimate=pl.CostEstimate(flops=20_000_000_000, bytes_accessed=1000, transcendentals=0),
        compiler_params=pltpu.CompilerParams(vmem_limit_bytes=46 << 20),
        name="parcel",
    )(facts, tiles)


SENDER = (0, X - 1, 1, 2)


def score_kernel(*refs, senders, items, arrays, tiles, length, group, chained, keep):
    s, n = len(senders), len(items)
    blocks, held, out = refs[:s], refs[s : s + arrays], refs[-2 if keep else -1]
    if keep:
        refs[-1][...] = blocks[-1][...]
    rows = tiles * length
    lane_group = lax.broadcasted_iota(jnp.int32, (8, 128), 1) // group
    row = lax.broadcasted_iota(jnp.int32, (8, 128), 0)
    core, x, z = lax.axis_index("core"), lax.axis_index("x"), lax.axis_index("z")
    best_of = [jnp.zeros((8, 128), jnp.float32)] * n
    for sender, queries in zip(senders, blocks):
        block = queries[...]
        here = lane_group == lax.rem(x + SENDER[sender], X)
        for i, (parcel, *_) in enumerate(items):
            similar = lax.dot_general(
                held[parcel][0:rows, :], block, (((1,), (1,)), ((), ())), preferred_element_type=jnp.float32
            )
            sums = []
            for t in range(tiles):
                best = jnp.max(similar[t * length : (t + 1) * length], axis=0, keepdims=True)
                sums.append(best[:, 0:128] + best[:, 128:256] + best[:, 256:384] + best[:, 384:512])
            sums = jnp.concatenate(sums + [jnp.zeros((8 - tiles, 128), jnp.float32)], axis=0)
            sums = sums + pltpu.roll(sums, 64, 1)
            sums = sums + pltpu.roll(sums, 32, 1)
            sums = sums + pltpu.roll(sums, 16, 1)
            best_of[i] = jnp.where(here, sums, best_of[i])

    found = [refs[s + arrays][c * Z : (c + 1) * Z] if chained else jnp.zeros((Z, 128), jnp.float32) for c in range(4)]
    way = 2 * core - 1
    for i, (_, label, steps, far) in enumerate(items):
        codes = held[label][rows : rows + 8 * X, :].astype(jnp.float32)
        code = jnp.full((8, 128), -1.0, jnp.float32)
        for d in range(X):
            turned = pltpu.roll(codes[d * 8 : d * 8 + 8], lax.rem((d - z) * group + 128, 128), 1)
            code = jnp.where(lane_group == d, turned, code)
        code = code.astype(jnp.int32) - tiles * (1 - core if far else core)
        shard = lax.rem(z + steps * way + Z, Z)
        for c in range(4):
            picked = (code[c : c + 1] == row) & (row < tiles)
            line = jnp.sum(jnp.where(picked, best_of[i], 0.0), axis=0, keepdims=True)
            found[c] = found[c] + jnp.where(row == shard, line, 0.0)
    for c in range(4):
        out[c * Z : (c + 1) * Z] = found[c]


def score(blocks, items, tiles, length, group, begun=None, keep=False):
    held = []

    def at(array):
        for i, one in enumerate(held):
            if one is array:
                return i
        held.append(array)
        return len(held) - 1

    plan = tuple((at(parcel), at(label), steps, far) for parcel, label, steps, far in items)
    more = [] if begun is None else [begun]
    shape = jax.ShapeDtypeStruct((4 * Z, 128), jnp.float32)
    return pl.pallas_call(
        functools.partial(
            score_kernel,
            senders=tuple(blocks),
            items=plan,
            arrays=len(held),
            tiles=tiles,
            length=length,
            group=group,
            chained=begun is not None,
            keep=keep,
        ),
        in_specs=[VM] * (len(blocks) + len(held) + len(more)),
        out_specs=[VM, VM] if keep else VM,
        out_shape=[shape, jax.ShapeDtypeStruct((512, 128), jnp.bfloat16)] if keep else shape,
        compiler_params=pltpu.CompilerParams(vmem_limit_bytes=32 << 20),
        cost_estimate=FREE,
        name=f"score_{len(blocks)}_{len(plan)}",
    )(*blocks.values(), *held, *more)


def finish_kernel(*refs, group):
    sources, out, table = refs[:4], refs[4], refs[5]
    x = lax.axis_index("x")
    for sender, source in zip(SENDER, sources):
        lines = pltpu.roll(source[...], lax.rem(128 - x * group, 128), 1)
        shard = lax.rem(x + sender, X) * Z
        for c in range(4):
            table[pl.ds(pl.multiple_of(c * X * Z + shard, Z), Z), :] = lines[c * Z : (c + 1) * Z]
    turned = table[...].T
    for c in range(4):
        out[:, c, :] = turned[0:group, c * X * Z : (c + 1) * X * Z]


def finish(sources, group):
    return pl.pallas_call(
        functools.partial(finish_kernel, group=group),
        in_specs=[VM] * 4,
        out_specs=VM,
        out_shape=jax.ShapeDtypeStruct((group, 4, X * Z), jnp.float32),
        scratch_shapes=[pltpu.VMEM((128, 128), jnp.float32)],
        compiler_params=pltpu.CompilerParams(vmem_limit_bytes=8 << 20),
        name="finish",
    )(*sources)


def tied(*arrays):
    return lax.optimization_barrier(arrays)


def shards(tokens, w_in, b_in, w_out, b_out, gain, shift, proj, tiles, lengths, slots, counts):
    queries, query_len, width = tokens.shape
    count, length, dims = tiles.shape
    half = count // CORES
    own, own_far = make_parcel(lengths, slots.transpose(1, 2, 0)[0], counts.transpose(1, 0), tiles)

    def along(a, k):
        ways = [(z, (z + k) % Z) for z in range(Z)] + [(Z + z, Z + (z - k) % Z) for z in range(Z)]
        return lax.ppermute(a, ("core", "z"), ways)

    def across(a, k):
        return lax.ppermute(a, "x", turn(X, k))

    def swap(a):
        return lax.ppermute(a, "core", turn(CORES, 1))

    near = {0: own} | {k: along(own, k) for k in (1, -1, 2, -2)}
    far = {0: own_far}
    flat, _ = tied(tokens.reshape(queries * query_len, width), own)
    embeds = encode(flat, w_in, b_in, w_out, b_out, gain, shift, proj, queries, query_len)
    near[1], near[-1], near[2], near[-2], embeds = tied(near[1], near[-1], near[2], near[-2], embeds)
    near[3], near[-3], near[4] = along(near[2], 1), along(near[-2], -1), along(near[2], 2)
    blocks = {i: across(embeds, k) for i, k in ((1, 1), (2, -1), (3, 2))} | {0: embeds}
    args = (half, length, queries)

    def mine(*ks):
        return [(near[k], near[k], k, False) for k in ks]

    def others(*ks):
        return [(far[k], near[k if k == 4 else -k], -k, True) for k in ks]

    early = mine(0, 1, -1, 2, -2) + others(0)
    found, blocks[0] = score({0: blocks[0]}, early, *args, keep=True)
    found, *ready = tied(found, *(near[k] for k in (1, -1, 2, -2)))
    far |= {k: swap(a) for k, a in zip((1, -1, 2, -2), ready)}
    found = score({i: blocks[i] for i in (1, 2, 3)}, early, *args, begun=found)
    found, near[3], near[-3], near[4] = tied(found, near[3], near[-3], near[4])
    far |= {k: swap(near[k]) for k in (3, -3, 4)}
    found = score(blocks, others(1, -1, 2, -2), *args, begun=found)
    found = score(blocks, mine(3, -3, 4) + others(3, -3, 4), *args, begun=found)
    sources = [found] + [across(found, k) for k in (1, -1, 2)]
    return finish(sources, queries).transpose(0, 2, 1)


def solution(mesh):
    fine = Mesh(mesh.devices.reshape(Y, CORES, X, Z), ("y", "core", "x", "z"))
    group, shard = ("y", "core"), ("x", "z")
    placed = (P(group + shard),) + (P(),) * 7 + (P(shard), P(shard), P(group, shard), P(group, shard))
    return jax.shard_map(shards, mesh=fine, in_specs=placed, out_specs=P(group + shard), check_vma=False)
```

```python
import functools

import jax
import jax.numpy as jnp
from jax import lax
from jax.experimental import pallas as pl
from jax.experimental.pallas import tpu as pltpu
from jax.sharding import Mesh
from jax.sharding import PartitionSpec as P

Y, CORES, X, Z = 4, 2, 4, 8
HALF_ROOT = 0.7071067811865476


def turn(size, step):
    return [(i, (i + step) % size) for i in range(size)]


def gelu(pre):
    return 0.5 * pre * (1.0 + lax.erf(pre * jnp.float32(HALF_ROOT)))


FREE = pl.CostEstimate(flops=1000, bytes_accessed=1000, transcendentals=0)


def ffn_kernel(tok, w_in, b_in, w_out, b_out, gain, shift, proj, out, acc, turned, *, queries, tokens):
    step = pl.program_id(0)
    chunk = w_in.shape[1]
    start = pl.multiple_of(step * chunk, chunk)
    pre = jnp.dot(tok[...], w_in[...], preferred_element_type=jnp.float32) + b_in[pl.ds(start, chunk)][None, :]
    hidden = gelu(pre).astype(jnp.bfloat16)
    part = jnp.dot(hidden, w_out[...], preferred_element_type=jnp.float32)

    @pl.when(step == 0)
    def _():
        acc[...] = part

    @pl.when(step > 0)
    def _():
        acc[...] += part

    @pl.when(step == pl.num_programs(0) - 1)
    def _():
        total = acc[...] + b_out[...][None, :] + tok[...].astype(jnp.float32)
        diff = total - jnp.mean(total, axis=-1, keepdims=True)
        spread = jnp.mean(diff * diff, axis=-1, keepdims=True)
        normed = (diff * lax.rsqrt(spread + 1e-5) * gain[...][None, :] + shift[...][None, :]).astype(jnp.bfloat16)
        projected = jnp.dot(normed, proj[...], preferred_element_type=jnp.float32)
        scale = lax.rsqrt(jnp.sum(projected * projected, axis=-1, keepdims=True) + 1e-6)
        embeds = projected * scale
        for q in range(queries):
            turned[pl.ds(q, tokens, stride=queries), :] = embeds[q * tokens : (q + 1) * tokens, :]
        out[...] = turned[...].astype(jnp.bfloat16)


def encode(tok, w_in, b_in, w_out, b_out, gain, shift, proj, queries, tokens, chunk=1536):
    rows, width = tok.shape

    def whole(a):
        return pl.BlockSpec(a.shape, lambda j: (0,) * a.ndim)

    return pl.pallas_call(
        functools.partial(ffn_kernel, queries=queries, tokens=tokens),
        grid=(w_in.shape[1] // chunk,),
        in_specs=[
            whole(tok),
            pl.BlockSpec((width, chunk), lambda j: (0, j)),
            whole(b_in),
            pl.BlockSpec((chunk, width), lambda j: (j, 0)),
            whole(b_out),
            whole(gain),
            whole(shift),
            whole(proj),
        ],
        out_specs=pl.BlockSpec((rows, proj.shape[1]), lambda j: (0, 0)),
        out_shape=jax.ShapeDtypeStruct((rows, proj.shape[1]), jnp.bfloat16),
        scratch_shapes=[pltpu.VMEM((rows, width), jnp.float32), pltpu.VMEM((rows, proj.shape[1]), jnp.float32)],
        compiler_params=pltpu.CompilerParams(vmem_limit_bytes=36 << 20),
        cost_estimate=FREE,
        name="encode",
    )(tok, w_in, b_in, w_out, b_out, gain, shift, proj)


VM = pl.BlockSpec(memory_space=pltpu.VMEM)


def parcel_kernel(facts, tiles, out, other, *, half):
    length = tiles.shape[1]
    core = lax.axis_index("core")
    column = lax.broadcasted_iota(jnp.int32, tiles.shape[1:], 0).astype(jnp.float32)
    lane = lax.broadcasted_iota(jnp.int32, (1, 128), 1)
    for side, to in ((core, out), (1 - core, other)):
        for t in range(half):
            tile = tiles[side * half + t].astype(jnp.float32)
            size = jnp.sum(jnp.where(lane == side * half + t, facts[4:5, 0:128], 0.0), axis=1, keepdims=True)
            to[t * length : (t + 1) * length, :] = jnp.where(column < size, tile, tile[0:1, :]).astype(jnp.bfloat16)
    lines = []
    for x in range(X):
        lines += [facts[0:4, x * 128 : (x + 1) * 128], jnp.zeros((4, 128), jnp.float32)]
    out[half * length : half * length + 8 * X, :] = jnp.concatenate(lines, axis=0).astype(jnp.bfloat16)


def make_parcel(sizes, slots, counts, tiles):
    count, length, dims = tiles.shape
    half = count // CORES
    order = jnp.arange(4, dtype=jnp.int32)[:, None]
    codes = jnp.where(order < counts, slots, count)
    facts = jnp.concatenate([codes, jnp.pad(sizes, (0, codes.shape[1] - count))[None, :]], axis=0).astype(jnp.float32)
    return pl.pallas_call(
        functools.partial(parcel_kernel, half=half),
        in_specs=[VM, VM],
        out_specs=[VM, VM],
        out_shape=[jax.ShapeDtypeStruct((half * length + r, dims), jnp.bfloat16) for r in (8 * X, 0)],
        cost_estimate=pl.CostEstimate(flops=20_000_000_000, bytes_accessed=1000, transcendentals=0),
        compiler_params=pltpu.CompilerParams(vmem_limit_bytes=46 << 20),
        name="parcel",
    )(facts, tiles)


SENDER = (0, X - 1, 1, 2)


def score_kernel(*refs, senders, items, arrays, tiles, length, group, chained, keep):
    s, n = len(senders), len(items)
    blocks, held, out = refs[:s], refs[s : s + arrays], refs[-2 if keep else -1]
    if keep:
        refs[-1][...] = blocks[-1][...]
    rows = tiles * length
    lane_group = lax.broadcasted_iota(jnp.int32, (8, 128), 1) // group
    row = lax.broadcasted_iota(jnp.int32, (8, 128), 0)
    core, x, z = lax.axis_index("core"), lax.axis_index("x"), lax.axis_index("z")
    best_of = [jnp.zeros((8, 128), jnp.float32)] * n
    for sender, queries in zip(senders, blocks):
        block = queries[...]
        here = lane_group == lax.rem(x + SENDER[sender], X)
        for i, (parcel, *_) in enumerate(items):
            similar = lax.dot_general(
                held[parcel][0:rows, :], block, (((1,), (1,)), ((), ())), preferred_element_type=jnp.float32
            )
            sums = []
            for t in range(tiles):
                best = jnp.max(similar[t * length : (t + 1) * length], axis=0, keepdims=True)
                sums.append(best[:, 0:128] + best[:, 128:256] + best[:, 256:384] + best[:, 384:512])
            sums = jnp.concatenate(sums + [jnp.zeros((8 - tiles, 128), jnp.float32)], axis=0)
            sums = sums + pltpu.roll(sums, 64, 1)
            sums = sums + pltpu.roll(sums, 32, 1)
            sums = sums + pltpu.roll(sums, 16, 1)
            best_of[i] = jnp.where(here, sums, best_of[i])

    found = [refs[s + arrays][c * Z : (c + 1) * Z] if chained else jnp.zeros((Z, 128), jnp.float32) for c in range(4)]
    way = 2 * core - 1
    for i, (_, label, steps, far) in enumerate(items):
        codes = held[label][rows : rows + 8 * X, :].astype(jnp.float32)
        code = jnp.full((8, 128), -1.0, jnp.float32)
        for d in range(X):
            turned = pltpu.roll(codes[d * 8 : d * 8 + 8], lax.rem((d - z) * group + 128, 128), 1)
            code = jnp.where(lane_group == d, turned, code)
        code = code.astype(jnp.int32) - tiles * (1 - core if far else core)
        shard = lax.rem(z + steps * way + Z, Z)
        for c in range(4):
            picked = (code[c : c + 1] == row) & (row < tiles)
            line = jnp.sum(jnp.where(picked, best_of[i], 0.0), axis=0, keepdims=True)
            found[c] = found[c] + jnp.where(row == shard, line, 0.0)
    for c in range(4):
        out[c * Z : (c + 1) * Z] = found[c]


def score(blocks, items, tiles, length, group, begun=None, keep=False):
    held = []

    def at(array):
        for i, one in enumerate(held):
            if one is array:
                return i
        held.append(array)
        return len(held) - 1

    plan = tuple((at(parcel), at(label), steps, far) for parcel, label, steps, far in items)
    more = [] if begun is None else [begun]
    shape = jax.ShapeDtypeStruct((4 * Z, 128), jnp.float32)
    return pl.pallas_call(
        functools.partial(
            score_kernel,
            senders=tuple(blocks),
            items=plan,
            arrays=len(held),
            tiles=tiles,
            length=length,
            group=group,
            chained=begun is not None,
            keep=keep,
        ),
        in_specs=[VM] * (len(blocks) + len(held) + len(more)),
        out_specs=[VM, VM] if keep else VM,
        out_shape=[shape, jax.ShapeDtypeStruct((512, 128), jnp.bfloat16)] if keep else shape,
        compiler_params=pltpu.CompilerParams(vmem_limit_bytes=32 << 20),
        cost_estimate=FREE,
        name=f"score_{len(blocks)}_{len(plan)}",
    )(*blocks.values(), *held, *more)


def finish_kernel(*refs, group):
    sources, out, table = refs[:4], refs[4], refs[5]
    x = lax.axis_index("x")
    for sender, source in zip(SENDER, sources):
        lines = pltpu.roll(source[...], lax.rem(128 - x * group, 128), 1)
        shard = lax.rem(x + sender, X) * Z
        for c in range(4):
            table[pl.ds(pl.multiple_of(c * X * Z + shard, Z), Z), :] = lines[c * Z : (c + 1) * Z]
    turned = table[...].T
    for c in range(4):
        out[:, c, :] = turned[0:group, c * X * Z : (c + 1) * X * Z]


def finish(sources, group):
    return pl.pallas_call(
        functools.partial(finish_kernel, group=group),
        in_specs=[VM] * 4,
        out_specs=VM,
        out_shape=jax.ShapeDtypeStruct((group, 4, X * Z), jnp.float32),
        scratch_shapes=[pltpu.VMEM((128, 128), jnp.float32)],
        compiler_params=pltpu.CompilerParams(vmem_limit_bytes=8 << 20),
        name="finish",
    )(*sources)


def tied(*arrays):
    return lax.optimization_barrier(arrays)


def shards(tokens, w_in, b_in, w_out, b_out, gain, shift, proj, tiles, lengths, slots, counts):
    queries, query_len, width = tokens.shape
    count, length, dims = tiles.shape
    half = count // CORES
    own, own_far = make_parcel(lengths, slots.transpose(1, 2, 0)[0], counts.transpose(1, 0), tiles)

    def along(a, k):
        ways = [(z, (z + k) % Z) for z in range(Z)] + [(Z + z, Z + (z - k) % Z) for z in range(Z)]
        return lax.ppermute(a, ("core", "z"), ways)

    def across(a, k):
        return lax.ppermute(a, "x", turn(X, k))

    def swap(a):
        return lax.ppermute(a, "core", turn(CORES, 1))

    near = {0: own} | {k: along(own, k) for k in (1, -1, 2, -2)}
    far = {0: own_far}
    flat, _ = tied(tokens.reshape(queries * query_len, width), own)
    embeds = encode(flat, w_in, b_in, w_out, b_out, gain, shift, proj, queries, query_len)
    near[2], near[-2], embeds = tied(near[2], near[-2], embeds)
    near[1], near[-1], near[2], near[-2] = tied(near[1], near[-1], near[2], near[-2])
    near[3], near[-3], near[4] = along(near[2], 1), along(near[-2], -1), along(near[2], 2)
    blocks = {i: across(embeds, k) for i, k in ((1, 1), (2, -1), (3, 2))} | {0: embeds}
    args = (half, length, queries)

    def mine(*ks):
        return [(near[k], near[k], k, False) for k in ks]

    def others(*ks):
        return [(far[k], near[k if k == 4 else -k], -k, True) for k in ks]

    early = mine(0, 1, -1, 2, -2) + others(0)
    found, blocks[0] = score({0: blocks[0]}, early, *args, keep=True)
    found, *ready = tied(found, *(near[k] for k in (1, -1, 2, -2)))
    far |= {k: swap(a) for k, a in zip((1, -1, 2, -2), ready)}
    found = score({i: blocks[i] for i in (1, 2, 3)}, early, *args, begun=found)
    found, near[3], near[-3], near[4] = tied(found, near[3], near[-3], near[4])
    far |= {k: swap(near[k]) for k in (3, -3, 4)}
    found = score(blocks, others(1, -1, 2, -2), *args, begun=found)
    found = score(blocks, mine(3, -3, 4) + others(3, -3, 4), *args, begun=found)
    sources = [found] + [across(found, k) for k in (1, -1, 2)]
    return finish(sources, queries).transpose(0, 2, 1)


def solution(mesh):
    fine = Mesh(mesh.devices.reshape(Y, CORES, X, Z), ("y", "core", "x", "z"))
    group, shard = ("y", "core"), ("x", "z")
    placed = (P(group + shard),) + (P(),) * 7 + (P(shard), P(shard), P(group, shard), P(group, shard))
    return jax.shard_map(shards, mesh=fine, in_specs=placed, out_specs=P(group + shard), check_vma=False)
```

```python
import functools

import jax
import jax.numpy as jnp
from jax import lax
from jax.experimental import pallas as pl
from jax.experimental.pallas import tpu as pltpu
from jax.sharding import Mesh
from jax.sharding import PartitionSpec as P

Y, CORES, X, Z = 4, 2, 4, 8
HALF_ROOT = 0.7071067811865476


def turn(size, step):
    return [(i, (i + step) % size) for i in range(size)]


def gelu(pre):
    return 0.5 * pre * (1.0 + lax.erf(pre * jnp.float32(HALF_ROOT)))


FREE = pl.CostEstimate(flops=1000, bytes_accessed=1000, transcendentals=0)


def ffn_kernel(tok, w_in, b_in, w_out, b_out, gain, shift, proj, out, acc, turned, *, queries, tokens):
    step = pl.program_id(0)
    chunk = w_in.shape[1]
    start = pl.multiple_of(step * chunk, chunk)
    pre = jnp.dot(tok[...], w_in[...], preferred_element_type=jnp.float32) + b_in[pl.ds(start, chunk)][None, :]
    hidden = gelu(pre).astype(jnp.bfloat16)
    part = jnp.dot(hidden, w_out[...], preferred_element_type=jnp.float32)

    @pl.when(step == 0)
    def _():
        acc[...] = part

    @pl.when(step > 0)
    def _():
        acc[...] += part

    @pl.when(step == pl.num_programs(0) - 1)
    def _():
        total = acc[...] + b_out[...][None, :] + tok[...].astype(jnp.float32)
        diff = total - jnp.mean(total, axis=-1, keepdims=True)
        spread = jnp.mean(diff * diff, axis=-1, keepdims=True)
        normed = (diff * lax.rsqrt(spread + 1e-5) * gain[...][None, :] + shift[...][None, :]).astype(jnp.bfloat16)
        projected = jnp.dot(normed, proj[...], preferred_element_type=jnp.float32)
        scale = lax.rsqrt(jnp.sum(projected * projected, axis=-1, keepdims=True) + 1e-6)
        embeds = projected * scale
        for q in range(queries):
            turned[pl.ds(q, tokens, stride=queries), :] = embeds[q * tokens : (q + 1) * tokens, :]
        out[...] = turned[...].astype(jnp.bfloat16)


def encode(tok, w_in, b_in, w_out, b_out, gain, shift, proj, queries, tokens, chunk=1024):
    rows, width = tok.shape

    def whole(a):
        return pl.BlockSpec(a.shape, lambda j: (0,) * a.ndim)

    return pl.pallas_call(
        functools.partial(ffn_kernel, queries=queries, tokens=tokens),
        grid=(w_in.shape[1] // chunk,),
        in_specs=[
            whole(tok),
            pl.BlockSpec((width, chunk), lambda j: (0, j)),
            whole(b_in),
            pl.BlockSpec((chunk, width), lambda j: (j, 0)),
            whole(b_out),
            whole(gain),
            whole(shift),
            whole(proj),
        ],
        out_specs=pl.BlockSpec((rows, proj.shape[1]), lambda j: (0, 0)),
        out_shape=jax.ShapeDtypeStruct((rows, proj.shape[1]), jnp.bfloat16),
        scratch_shapes=[pltpu.VMEM((rows, width), jnp.float32), pltpu.VMEM((rows, proj.shape[1]), jnp.float32)],
        compiler_params=pltpu.CompilerParams(vmem_limit_bytes=36 << 20),
        cost_estimate=FREE,
        name="encode",
    )(tok, w_in, b_in, w_out, b_out, gain, shift, proj)


VM = pl.BlockSpec(memory_space=pltpu.VMEM)


def parcel_kernel(facts, tiles, out, other, *, half):
    length = tiles.shape[1]
    core = lax.axis_index("core")
    column = lax.broadcasted_iota(jnp.int32, tiles.shape[1:], 0).astype(jnp.float32)
    lane = lax.broadcasted_iota(jnp.int32, (1, 128), 1)
    for side, to in ((core, out), (1 - core, other)):
        for t in range(half):
            tile = tiles[side * half + t].astype(jnp.float32)
            size = jnp.sum(jnp.where(lane == side * half + t, facts[4:5, 0:128], 0.0), axis=1, keepdims=True)
            to[t * length : (t + 1) * length, :] = jnp.where(column < size, tile, tile[0:1, :]).astype(jnp.bfloat16)
    lines = []
    for x in range(X):
        lines += [facts[0:4, x * 128 : (x + 1) * 128], jnp.zeros((4, 128), jnp.float32)]
    out[half * length : half * length + 8 * X, :] = jnp.concatenate(lines, axis=0).astype(jnp.bfloat16)


def make_parcel(sizes, slots, counts, tiles):
    count, length, dims = tiles.shape
    half = count // CORES
    order = jnp.arange(4, dtype=jnp.int32)[:, None]
    codes = jnp.where(order < counts, slots, count)
    facts = jnp.concatenate([codes, jnp.pad(sizes, (0, codes.shape[1] - count))[None, :]], axis=0).astype(jnp.float32)
    return pl.pallas_call(
        functools.partial(parcel_kernel, half=half),
        in_specs=[VM, VM],
        out_specs=[VM, VM],
        out_shape=[jax.ShapeDtypeStruct((half * length + r, dims), jnp.bfloat16) for r in (8 * X, 0)],
        cost_estimate=pl.CostEstimate(flops=20_000_000_000, bytes_accessed=1000, transcendentals=0),
        compiler_params=pltpu.CompilerParams(vmem_limit_bytes=46 << 20),
        name="parcel",
    )(facts, tiles)


SENDER = (0, X - 1, 1, 2)


def score_kernel(*refs, senders, items, arrays, tiles, length, group, chained, keep):
    s, n = len(senders), len(items)
    blocks, held, out = refs[:s], refs[s : s + arrays], refs[-2 if keep else -1]
    if keep:
        refs[-1][...] = blocks[-1][...]
    rows = tiles * length
    lane_group = lax.broadcasted_iota(jnp.int32, (8, 128), 1) // group
    row = lax.broadcasted_iota(jnp.int32, (8, 128), 0)
    core, x, z = lax.axis_index("core"), lax.axis_index("x"), lax.axis_index("z")
    best_of = [jnp.zeros((8, 128), jnp.float32)] * n
    for sender, queries in zip(senders, blocks):
        block = queries[...]
        here = lane_group == lax.rem(x + SENDER[sender], X)
        for i, (parcel, *_) in enumerate(items):
            similar = lax.dot_general(
                held[parcel][0:rows, :], block, (((1,), (1,)), ((), ())), preferred_element_type=jnp.float32
            )
            sums = []
            for t in range(tiles):
                best = jnp.max(similar[t * length : (t + 1) * length], axis=0, keepdims=True)
                sums.append(best[:, 0:128] + best[:, 128:256] + best[:, 256:384] + best[:, 384:512])
            sums = jnp.concatenate(sums + [jnp.zeros((8 - tiles, 128), jnp.float32)], axis=0)
            sums = sums + pltpu.roll(sums, 64, 1)
            sums = sums + pltpu.roll(sums, 32, 1)
            sums = sums + pltpu.roll(sums, 16, 1)
            best_of[i] = jnp.where(here, sums, best_of[i])

    found = [refs[s + arrays][c * Z : (c + 1) * Z] if chained else jnp.zeros((Z, 128), jnp.float32) for c in range(4)]
    way = 2 * core - 1
    for i, (_, label, steps, far) in enumerate(items):
        codes = held[label][rows : rows + 8 * X, :].astype(jnp.float32)
        code = jnp.full((8, 128), -1.0, jnp.float32)
        for d in range(X):
            turned = pltpu.roll(codes[d * 8 : d * 8 + 8], lax.rem((d - z) * group + 128, 128), 1)
            code = jnp.where(lane_group == d, turned, code)
        code = code.astype(jnp.int32) - tiles * (1 - core if far else core)
        shard = lax.rem(z + steps * way + Z, Z)
        for c in range(4):
            picked = (code[c : c + 1] == row) & (row < tiles)
            line = jnp.sum(jnp.where(picked, best_of[i], 0.0), axis=0, keepdims=True)
            found[c] = found[c] + jnp.where(row == shard, line, 0.0)
    for c in range(4):
        out[c * Z : (c + 1) * Z] = found[c]


def score(blocks, items, tiles, length, group, begun=None, keep=False):
    held = []

    def at(array):
        for i, one in enumerate(held):
            if one is array:
                return i
        held.append(array)
        return len(held) - 1

    plan = tuple((at(parcel), at(label), steps, far) for parcel, label, steps, far in items)
    more = [] if begun is None else [begun]
    shape = jax.ShapeDtypeStruct((4 * Z, 128), jnp.float32)
    return pl.pallas_call(
        functools.partial(
            score_kernel,
            senders=tuple(blocks),
            items=plan,
            arrays=len(held),
            tiles=tiles,
            length=length,
            group=group,
            chained=begun is not None,
            keep=keep,
        ),
        in_specs=[VM] * (len(blocks) + len(held) + len(more)),
        out_specs=[VM, VM] if keep else VM,
        out_shape=[shape, jax.ShapeDtypeStruct((512, 128), jnp.bfloat16)] if keep else shape,
        compiler_params=pltpu.CompilerParams(vmem_limit_bytes=32 << 20),
        cost_estimate=FREE,
        name=f"score_{len(blocks)}_{len(plan)}",
    )(*blocks.values(), *held, *more)


def finish_kernel(*refs, group):
    sources, out, table = refs[:4], refs[4], refs[5]
    x = lax.axis_index("x")
    for sender, source in zip(SENDER, sources):
        lines = pltpu.roll(source[...], lax.rem(128 - x * group, 128), 1)
        shard = lax.rem(x + sender, X) * Z
        for c in range(4):
            table[pl.ds(pl.multiple_of(c * X * Z + shard, Z), Z), :] = lines[c * Z : (c + 1) * Z]
    turned = table[...].T
    for c in range(4):
        out[:, c, :] = turned[0:group, c * X * Z : (c + 1) * X * Z]


def finish(sources, group):
    return pl.pallas_call(
        functools.partial(finish_kernel, group=group),
        in_specs=[VM] * 4,
        out_specs=VM,
        out_shape=jax.ShapeDtypeStruct((group, 4, X * Z), jnp.float32),
        scratch_shapes=[pltpu.VMEM((128, 128), jnp.float32)],
        compiler_params=pltpu.CompilerParams(vmem_limit_bytes=8 << 20),
        name="finish",
    )(*sources)


def tied(*arrays):
    return lax.optimization_barrier(arrays)


def shards(tokens, w_in, b_in, w_out, b_out, gain, shift, proj, tiles, lengths, slots, counts):
    queries, query_len, width = tokens.shape
    count, length, dims = tiles.shape
    half = count // CORES
    own, own_far = make_parcel(lengths, slots.transpose(1, 2, 0)[0], counts.transpose(1, 0), tiles)

    def along(a, k):
        ways = [(z, (z + k) % Z) for z in range(Z)] + [(Z + z, Z + (z - k) % Z) for z in range(Z)]
        return lax.ppermute(a, ("core", "z"), ways)

    def across(a, k):
        return lax.ppermute(a, "x", turn(X, k))

    def swap(a):
        return lax.ppermute(a, "core", turn(CORES, 1))

    near = {0: own} | {k: along(own, k) for k in (1, -1, 2, -2)}
    far = {0: own_far}
    flat, _ = tied(tokens.reshape(queries * query_len, width), own)
    embeds = encode(flat, w_in, b_in, w_out, b_out, gain, shift, proj, queries, query_len)
    near[2], near[-2], embeds = tied(near[2], near[-2], embeds)
    near[1], near[-1], near[2], near[-2] = tied(near[1], near[-1], near[2], near[-2])
    near[3], near[-3], near[4] = along(near[2], 1), along(near[-2], -1), along(near[2], 2)
    blocks = {i: across(embeds, k) for i, k in ((1, 1), (2, -1), (3, 2))} | {0: embeds}
    args = (half, length, queries)

    def mine(*ks):
        return [(near[k], near[k], k, False) for k in ks]

    def others(*ks):
        return [(far[k], near[k if k == 4 else -k], -k, True) for k in ks]

    early = mine(0, 1, -1, 2, -2) + others(0)
    found, blocks[0] = score({0: blocks[0]}, early, *args, keep=True)
    found, *ready = tied(found, *(near[k] for k in (1, -1, 2, -2)))
    far |= {k: swap(a) for k, a in zip((1, -1, 2, -2), ready)}
    found = score({i: blocks[i] for i in (1, 2, 3)}, early, *args, begun=found)
    found, near[3], near[-3], near[4] = tied(found, near[3], near[-3], near[4])
    far |= {k: swap(near[k]) for k in (3, -3, 4)}
    found = score(blocks, others(1, -1, 2, -2), *args, begun=found)
    found = score(blocks, mine(3, -3, 4) + others(3, -3, 4), *args, begun=found)
    sources = [found] + [across(found, k) for k in (1, -1, 2)]
    return finish(sources, queries).transpose(0, 2, 1)


def solution(mesh):
    fine = Mesh(mesh.devices.reshape(Y, CORES, X, Z), ("y", "core", "x", "z"))
    group, shard = ("y", "core"), ("x", "z")
    placed = (P(group + shard),) + (P(),) * 7 + (P(shard), P(shard), P(group, shard), P(group, shard))
    return jax.shard_map(shards, mesh=fine, in_specs=placed, out_specs=P(group + shard), check_vma=False)
```
